128 devices in a mesh: grid: 32 (over y, x, core), ao: 4 (over z).
Axes of the slice: x: 4, y: 4, z: 4, core: 2. Of those that a mesh axis runs over, the one named last changes fastest.
Arguments:
- colloc: bfloat16 [128, 128, 1024], P('grid', None, 'ao'), may hold values from -6 to 6
- potent: bfloat16 [128, 128, 1024], P('grid', None, 'ao'), may hold values from -6 to 6
- weights: float32 [128, 128], P('grid'), may hold values from 0.02 to 0.2
- density: bfloat16 [8192, 8192], P('grid'), may hold values from -0.1875 to 0.1875
- list_owner: int32 [128, 8], replicated, may hold values from 0 to 31, as said below
- list_local: int32 [128, 8], replicated, may hold values from 0 to 1
Outputs:
- exchange: float32 [8192, 8192], P('grid', 'ao')
The draws below stay inside these ranges and needn't reach their ends.
Inputs may be any that keep to these rules, and one draw needn't show every extreme that they name: `list_owner`: each row names 8 different owners. Among the 4 rows of one index of grid (rows d * 4 to (d + 1) * 4 - 1), no owner is named by more than 2 rows.
All inputs are finite; a program needn't handle non-finite values.
Results may differ from the reference program's by a relative error of at most 0.0029.
Values may be sent and summed in bfloat16 or wider, within the bound.
A program may use at most 64 MiB of HBM per device.

```python
import math
import jax
import jax.numpy as jnp
from jax import lax

PTS = 128
RBS = 128
SIG = 8
RB_PER = 2
BLK_DEV = 4
NBLK = 128
NAO = 8192


def draw_list_owner(key, part):
    key = jax.random.fold_in(key, 11)
    n_grid = NBLK // BLK_DEV
    capacity = min(BLK_DEV, 2 * ((BLK_DEV * SIG + n_grid - 1) // n_grid))
    others = n_grid - 1
    skip_most = 1 if others >= 2 * SIG else 0
    seq_len = BLK_DEV * SIG - capacity
    key_hot, key_perm, key_skip, key_start, key_order, key_slot = jax.random.split(key, 6)
    hottest = jax.random.randint(key_hot, (), 0, n_grid)
    perms = jax.vmap(lambda k: jax.random.permutation(k, others))(jax.random.split(key_perm, n_grid))
    skips = jax.random.randint(key_skip, (n_grid, seq_len), 0, skip_most + 1)
    starts = jax.random.randint(key_start, (n_grid, 1), 0, others)
    spots = jnp.arange(seq_len, dtype=jnp.int32)[None, :] + jnp.cumsum(skips, axis=1) - skips
    residue = (starts + spots) % others
    picked = jnp.take_along_axis(perms, residue, axis=1)
    picked = jnp.where(picked >= hottest, picked + 1, picked)
    ranks = jnp.arange(BLK_DEV, dtype=jnp.int32)
    has_hot = (ranks < capacity).astype(jnp.int32)
    offset = ranks * SIG - jnp.minimum(ranks, capacity)
    slots = jnp.arange(SIG, dtype=jnp.int32)
    seq_index = jnp.clip(offset[:, None] + slots[None, :] - has_hot[:, None], 0, seq_len - 1)
    entries = picked[:, seq_index]
    is_hot = (has_hot[:, None] == 1) & (slots[None, :] == 0)
    entries = jnp.where(is_hot[None, :, :], hottest, entries)
    order = jax.vmap(lambda k: jax.random.permutation(k, BLK_DEV))(jax.random.split(key_order, n_grid))
    entries = jnp.take_along_axis(entries, order[:, :, None], axis=1)
    slot_keys = jax.random.split(key_slot, n_grid * BLK_DEV)
    slot_perm = jax.vmap(lambda k: jax.random.permutation(k, SIG))(slot_keys).reshape(n_grid, BLK_DEV, SIG)
    entries = jnp.take_along_axis(entries, slot_perm, axis=2)
    return entries.reshape(NBLK, SIG).astype(jnp.int32)


def set_ends(values, own_key, smallest, high):
    index_at = [jax.random.randint(jax.random.fold_in(own_key, axis), (), 0, length) for axis, length in enumerate(values.shape)]
    main_axis = values.shape.index(max(values.shape))
    beside = index_at[:main_axis] + [(index_at[main_axis] + 1) % values.shape[main_axis]] + index_at[main_axis + 1:]
    return values.at[tuple(index_at)].set(smallest).at[tuple(beside)].set(high)


def levels(key, dims, cuts, low, top_value):
    level = 1.0
    for position, parts in cuts:
        steps = jax.random.uniform(jax.random.fold_in(jax.random.fold_in(key, 6), position), (parts,), jnp.float32, low / len(cuts), top_value / len(cuts))
        level = level * jnp.repeat(jnp.exp(steps), dims[position] // parts).reshape((-1,) + (1,) * (len(dims) - 1 - position))
    return level


def gaussian(rng, shape, scale, limit, cuts=(), kind=jnp.bfloat16):
    drawn = scale * jax.random.normal(rng, shape, jnp.float32)
    if cuts:
        drawn = drawn * levels(rng, shape, cuts, -0.22, 0.18)
    return jnp.clip(drawn, -limit, limit).astype(kind)


def setup_inputs(seed: int = 0) -> dict:
    keys = jax.random.split(jax.random.key(seed), 7)
    colloc = gaussian(keys[0], (NBLK, PTS, SIG * RBS), 1.0, 6.0, ((0, 32), (2, 4)))
    potent = gaussian(keys[1], (NBLK, PTS, SIG * RBS), 1.0, 6.0, ((0, 32), (2, 4)))
    weights = jnp.clip(jnp.exp(math.log(0.2) - 2.3025851 * jax.random.uniform(keys[2], (NBLK, PTS), jnp.float32) ** levels(keys[2], (NBLK, PTS), ((0, 32),), -0.2, 0.2)), 0.02, 0.2)
    density = gaussian(keys[3], (NAO, NAO), (SIG * RBS) ** -0.5, 0.1875, ((0, 32),))
    list_owner = draw_list_owner(jax.random.fold_in(keys[6], 71), 0)
    list_local = set_ends(jax.random.randint(keys[5], (NBLK, SIG), 0, RB_PER), jax.random.fold_in(keys[5], 1), 0, RB_PER - 1).astype(jnp.int32)
    return {"colloc": colloc, "potent": potent, "weights": weights, "density": density, "list_owner": list_owner, "list_local": list_local}


def reference(colloc, potent, weights, density, list_owner, list_local):
    n_rows = density.shape[0] // RBS
    row_ids = (list_owner * RB_PER + list_local).astype(jnp.int32)
    blocked = density.reshape(n_rows, RBS, n_rows, RBS)

    def step(totals, item):
        block_colloc, block_pot, block_weights, ids = item
        tiles = blocked[ids[:, None], :, ids[None, :], :]
        gathered = jnp.transpose(tiles, (0, 2, 1, 3)).reshape(SIG * RBS, SIG * RBS)
        f_vals = jnp.dot(block_colloc, gathered, preferred_element_type=jnp.float32)
        weighted = (block_weights[:, None] * block_pot * f_vals).astype(jnp.bfloat16)
        partial_sum = jnp.dot(block_colloc.T, weighted, preferred_element_type=jnp.float32)
        pieces = jnp.transpose(partial_sum.reshape(SIG, RBS, SIG, RBS), (0, 2, 1, 3))
        return totals.at[ids[:, None], :, ids[None, :], :].add(pieces), None

    start = jnp.zeros((n_rows, RBS, n_rows, RBS), jnp.float32)
    totals, unused = lax.scan(step, start, (colloc, potent, weights, row_ids))
    return totals.reshape(n_rows * RBS, n_rows * RBS)
```

```python
import functools

import jax
import jax.numpy as jnp
from jax import lax
from jax.experimental import pallas as pl
from jax.experimental.pallas import tpu as pltpu
from jax.sharding import PartitionSpec as P

RBS = 128
SIG = 8
BLK = 4
NG = 32
NA = 4
NY = 4
NX = 4
CAP = 2
TILES = 16
N_COL = 64
MESH = pl.DeviceIdType.MESH
F32 = jnp.float32
BF16 = jnp.bfloat16

T_K0 = 0
T_K1 = T_K0 + NG * CAP
T_ARR = T_K1 + NG * CAP
T_CB = T_ARR + BLK * SIG
T_SEL = T_CB + NG * CAP
T_IDX = T_SEL + TILES
T_END = T_IDX + NG * CAP * TILES

OFFSETS = sorted(
    [(oy, ox, oc) for oy in range(NY) for ox in range(NX) for oc in range(2) if (oy, ox, oc) != (0, 0, 0)],
    key=lambda o: -(min(o[0], NY - o[0]) + min(o[1], NX - o[1])),
)


def plan(list_owner, list_local, me, part):
    owners = list_owner.reshape(NG, BLK, SIG)
    local_rows = list_local.reshape(NG, BLK, SIG)
    row_ids = owners * 2 + local_rows
    i32 = jnp.int32
    places = jnp.arange(CAP, dtype=i32)
    lower = (jnp.arange(BLK)[:, None] > jnp.arange(BLK)[None, :]).astype(i32)

    hit = (owners == me).astype(i32)
    named = jnp.sum(hit, axis=2)
    before = jnp.sum(named[:, None, :] * lower[None], axis=2)
    chosen = named[:, None, :] * (before[:, None, :] == places[None, :, None]).astype(i32)
    valid = jnp.sum(chosen, axis=2)
    row = jnp.sum(chosen * jnp.sum(hit * local_rows, axis=2)[:, None, :], axis=2)
    my_cols = lax.dynamic_slice_in_dim(row_ids, part * 2, 2, axis=2)
    cols = jnp.sum(chosen[:, :, :, None] * my_cols[:, None], axis=2)
    keep = (valid[:, :, None] * (row[:, :, None] == jnp.arange(2, dtype=i32))).astype(F32)

    mine = lax.dynamic_index_in_dim(owners, me, 0, keepdims=False)
    mine_named = jnp.sum((mine[:, :, None] == jnp.arange(NG, dtype=i32)).astype(i32), axis=1)
    mine_before = jnp.sum(mine_named[None] * lower[:, :, None], axis=1)
    same = (mine[:, :, None] == jnp.arange(NG, dtype=i32)).astype(i32)
    spot = jnp.sum(same * mine_before[:, None, :], axis=2)
    arr = mine * CAP + spot

    pick = mine_named[None] * (mine_before[None] == places[:, None, None]).astype(i32)
    cb = jnp.sum(pick * jnp.arange(BLK, dtype=i32)[None, :, None], axis=1)
    slot = jnp.sum(same * jnp.arange(SIG, dtype=i32)[None, :, None], axis=1)
    cj = jnp.sum(pick * slot[None], axis=1)
    cb = (cj // 2) * (2 * BLK) + cb * 2 + cj % 2

    group = (owners // (NG // NA) == part).astype(i32).reshape(NG, BLK * SIG)
    n = BLK * SIG
    below = (jnp.arange(n)[:, None] > jnp.arange(n)[None, :]).astype(i32)
    rank = jnp.sum(group[:, None, :] * below[None], axis=2)
    my_group = lax.dynamic_index_in_dim(group, me, 0, keepdims=False)
    my_rank = lax.dynamic_index_in_dim(rank, me, 0, keepdims=False)
    flat = jnp.arange(n, dtype=i32)
    b_of, k_of = flat // SIG, flat % SIG
    stored = (k_of // 2) * (2 * BLK) + b_of * 2 + k_of % 2
    tiles = jnp.arange(TILES, dtype=i32)
    sel = jnp.sum(my_group[None] * (my_rank[None] == tiles[:, None]).astype(i32) * stored[None], axis=1)

    here = (row_ids[:, :, :, None] == part * TILES + tiles).astype(i32)
    at = jnp.sum(here * (rank.reshape(NG, BLK, SIG)[..., None] - TILES), axis=2)
    idx = TILES + jnp.sum(chosen[..., None] * at[:, None], axis=2)

    tab = jnp.concatenate(
        [
            (row * N_COL + cols[:, :, 0]).reshape(-1),
            (row * N_COL + cols[:, :, 1]).reshape(-1),
            arr.reshape(-1),
            cb.T.reshape(-1),
            sel,
            idx.reshape(-1),
        ]
    )
    return tab, keep.reshape(-1)


def kernel(tab, keep, colloc, potent, weights, dens, out, dtiles, send, arrived, cfull, cqs, cown, wz, lhs_t, picked, *rest):
    held = rest[: NG]
    dsend, drecv, csend, crecv, zsend, zrecv, gsend, grecv = rest[NG:]
    me = lax.axis_index("grid")
    part = lax.axis_index("ao")
    y = me // (2 * NX)
    x = (me // 2) % NX
    core = me % 2

    def at_offset(oy, ox, oc):
        return ((y + oy + NY) % NY) * (2 * NX) + ((x + ox + NX) % NX) * 2 + (core + oc) % 2

    barrier = pltpu.get_barrier_semaphore()
    for o in OFFSETS:
        pl.semaphore_signal(barrier, inc=1, device_id=(at_offset(*o), part), device_id_type=MESH)
    for o in range(1, NA):
        pl.semaphore_signal(barrier, inc=1, device_id=(me, (part + o) % NA), device_id_type=MESH)

    def pack(d, carry):
        for c in range(CAP):
            i = d * CAP + c
            for h, base in enumerate((T_K0, T_K1)):
                send[i, :, h * RBS : (h + 1) * RBS] = dtiles[tab[base + i]]
        return carry

    for r in range(2):
        for k in range(N_COL):
            dtiles[r * N_COL + k] = dens[r * RBS : (r + 1) * RBS, k * RBS : (k + 1) * RBS]
    lax.fori_loop(0, NG, pack, 0)
    for b in range(BLK):
        for h in range(2):
            cfull[part * 2 * BLK + 2 * b + h] = colloc[b, :, h * RBS : (h + 1) * RBS]
    pl.semaphore_wait(barrier, len(OFFSETS) + NA - 1)

    def z_copy(buf, base, o, there):
        count = buf.shape[0] // NA
        return pltpu.make_async_remote_copy(
            src_ref=buf.at[pl.ds(part * count, count)],
            dst_ref=buf.at[pl.ds(there * count, count)],
            send_sem=zsend.at[base + o - 1],
            recv_sem=zrecv.at[base + o - 1],
            device_id=(me, (part + o) % NA),
            device_id_type=MESH,
        )

    def z_start(buf, base):
        for o in (2, 1, 3):
            z_copy(buf, base, o, part).start()

    def z_wait_recv(buf, base):
        for o in (1, 3, 2):
            z_copy(buf, base, o, (part + NA - o) % NA).wait_recv()

    def z_wait_send(buf, base):
        for o in (1, 2, 3):
            z_copy(buf, base, o, part).wait_send()

    def d_copy(n, c, recv):
        oy, ox, oc = OFFSETS[n]
        to = at_offset(oy, ox, oc)
        frm = at_offset(-oy, -ox, oc) if recv else me
        return pltpu.make_async_remote_copy(
            src_ref=send.at[to * CAP + c],
            dst_ref=arrived.at[frm * CAP + c],
            send_sem=dsend.at[n * CAP + c],
            recv_sem=drecv.at[n * CAP + c],
            device_id=(to, part),
            device_id_type=MESH,
        )

    def c_copy(n, recv):
        oy, ox, oc = OFFSETS[n]
        to = at_offset(oy, ox, oc)
        frm = at_offset(-oy, -ox, oc) if recv else me
        return pltpu.make_async_remote_copy(
            src_ref=cqs.at[to],
            dst_ref=cown.at[part * NG + frm],
            send_sem=csend.at[n],
            recv_sem=crecv.at[n],
            device_id=(to, part),
            device_id_type=MESH,
        )

    z_start(cfull, 0)
    for n in range(NG - 1):
        d_copy(n, 0, False).start()
    for c in range(CAP):
        arrived[me * CAP + c] = send[me * CAP + c]

    z_wait_recv(cfull, 0)
    quarter = RBS // NA

    def pack_c(o, carry):
        for c in range(CAP):
            picked[...] = cfull[tab[T_CB + o * CAP + c]]
            rows = pl.multiple_of(part * quarter, quarter)
            cqs[o, c] = picked[pl.ds(rows, quarter), :]
        return carry

    lax.fori_loop(0, NG, pack_c, 0)
    for n in range(NG - 1):
        c_copy(n, False).start()
    for n in range(NG - 1):
        d_copy(n, 1, False).start()
    cown[part * NG + me] = cqs[me]
    for s in range(NG):
        held[s][TILES] = jnp.zeros((RBS, RBS), BF16)
    for n in range(NG - 1):
        c_copy(n, True).wait_recv()
    z_start(cown, 3)
    for c in range(CAP):
        for n in range(NG - 1):
            d_copy(n, c, True).wait_recv()

    for b in range(BLK):
        left = jnp.concatenate([cfull[q * 2 * BLK + 2 * b + h] for q in range(NA) for h in range(2)], axis=1)
        right = jnp.concatenate([arrived[tab[T_ARR + b * SIG + j]] for j in range(SIG)], axis=0)
        f_vals = jnp.dot(left, right, preferred_element_type=F32)
        w = jnp.transpose(jnp.broadcast_to(weights[b : b + 1, :], (RBS, RBS)))
        for h in range(2):
            cut = slice(h * RBS, (h + 1) * RBS)
            wz[part * 2 * BLK + 2 * b + h] = (w * potent[b, :, cut].astype(F32) * f_vals[:, cut]).astype(BF16)
    z_start(wz, 6)

    z_wait_recv(cown, 3)

    def build(d, carry):
        for c in range(CAP):
            tile = jnp.concatenate([cown[q * NG + d, c].astype(F32) for q in range(NA)], axis=0)
            tile = jnp.transpose(tile)
            for r in range(2):
                lhs_t[d, r * RBS : (r + 1) * RBS, c * RBS : (c + 1) * RBS] = (
                    tile * keep[(d * CAP + c) * 2 + r]
                ).astype(BF16)
        return carry

    lax.fori_loop(0, NG, build, 0)
    out[...] = jnp.zeros_like(out)
    z_wait_recv(wz, 6)

    def piece(oy, ox, oc=0):
        return held[((oy % NY) * NX + ox % NX) * 2 + oc]

    own = piece(0, 0)
    for t in range(TILES):
        own[t] = wz[tab[T_SEL + t]]

    moves = {}

    def move(key, oy, ox, low, count, dy, dx, dc=0):
        n = len(moves)
        rows = pl.ds(low, count)
        copy = pltpu.make_async_remote_copy(
            src_ref=piece(oy, ox).at[rows],
            dst_ref=piece(oy + dy, ox + dx, dc).at[rows],
            send_sem=gsend.at[n],
            recv_sem=grecv.at[n],
            device_id=(at_offset(dy, dx, dc), part),
            device_id_type=MESH,
        )
        moves[key] = copy
        copy.start()

    first = ((0, 1), (1, 0))
    second = ((1, 0), (0, 1))
    half = TILES // 2

    def along(h, i, s=0):
        (py, px), (qy, qx) = first[h], second[h]
        return (i * py + s * qy, i * px + s * qx)

    def send_first(h):
        for s in (1, -1):
            move(("p", h, s), 0, 0, h * half, half, *along(h, s))

    def send_second(h, i):
        for s in (1, -1):
            move(("q", h, i, s), *along(h, i), h * half, half, *along(h, 0, s))

    def split(h, s):
        return h * half + (0 if s > 0 else half // 2), half // 2

    def forward_first(h, s):
        moves["p", h, s].wait_recv()
        move(("pf", h, s), *along(h, s), *split(h, s), *along(h, s))

    def forward_second(h, i, s):
        moves["q", h, i, s].wait_recv()
        move(("qf", h, i, s), *along(h, i, s), *split(h, s), *along(h, 0, s))

    def to_sibling(oy, ox):
        move(("s", oy % NY, ox % NX), oy, ox, 0, TILES, 0, 0, 1)

    def add_piece(oy, ox, oc):
        src = at_offset(-oy, -ox, oc)
        buf = piece(oy, ox, oc)
        width = 4

        def step(m, carry):
            tiles = []
            for c in range(CAP):
                base = T_IDX + (src * CAP + c) * TILES + m * width
                tiles.append(jnp.concatenate([buf[tab[base + w]] for w in range(width)], axis=1))
            right = jnp.concatenate(tiles, axis=0)
            cols = pl.ds(pl.multiple_of(m * width * RBS, width * RBS), width * RBS)
            out[:, cols] += jnp.dot(lhs_t[src], right, preferred_element_type=F32)
            return carry

        lax.fori_loop(0, TILES // width, step, 0)

    def finish(pieces):
        for oy, ox in pieces:
            to_sibling(oy, ox)

    def add(pieces, oc):
        for oy, ox in pieces:
            if oc:
                moves["s", oy % NY, ox % NX].wait_recv()
            add_piece(oy, ox, oc)

    for h in range(2):
        send_first(h)
    for h in range(2):
        send_second(h, 0)
    to_sibling(0, 0)
    add([(0, 0)], 0)
    for s in (1, -1):
        for h in range(2):
            forward_first(h, s)
            send_second(h, s)
    for s in (1, -1):
        for h in range(2):
            forward_second(h, 0, s)
    near = [(0, 1), (0, -1), (1, 0), (-1, 0)]
    finish(near)
    for h in range(2):
        for s in (1, -1):
            moves["pf", h, s].wait_recv()
        send_second(h, 2)
    add([(0, 0)], 1)
    add(near, 0)
    diagonal = [(1, 1), (1, -1), (-1, 1), (-1, -1)]
    for i in (1, -1):
        for s in (1, -1):
            for h in range(2):
                forward_second(h, i, s)
    finish(diagonal)
    for h in range(2):
        for s in (1, -1):
            moves["qf", h, 0, s].wait_recv()
    straight = [(0, 2), (2, 0)]
    finish(straight)
    add(near, 1)
    add(diagonal, 0)
    for s in (1, -1):
        for h in range(2):
            forward_second(h, 2, s)
    add(straight, 0)
    add(diagonal, 1)
    for i in (1, -1):
        for h in range(2):
            for s in (1, -1):
                moves["qf", h, i, s].wait_recv()
    knight = [(1, 2), (-1, 2), (2, 1), (2, -1)]
    finish(knight)
    add(straight, 1)
    add(knight, 0)
    for h in range(2):
        for s in (1, -1):
            moves["qf", h, 2, s].wait_recv()
    last = [(2, 2)]
    finish(last)
    add(knight, 1)
    add(last, 0)
    add(last, 1)

    for n in range(NG - 1):
        for c in range(CAP):
            d_copy(n, c, False).wait_send()
        c_copy(n, False).wait_send()
    z_wait_send(cfull, 0)
    z_wait_send(cown, 3)
    z_wait_send(wz, 6)
    for copy in moves.values():
        copy.wait_send()


def local(colloc, potent, weights, density, list_owner, list_local):
    me = lax.axis_index("grid")
    part = lax.axis_index("ao")
    tab, keep = plan(list_owner, list_local, me, part)
    smem = pl.BlockSpec(memory_space=pltpu.SMEM)
    vmem = pl.BlockSpec(memory_space=pltpu.VMEM)
    dma = pltpu.SemaphoreType.DMA
    return pl.pallas_call(
        kernel,
        out_shape=jax.ShapeDtypeStruct((2 * RBS, TILES * RBS), F32),
        in_specs=[smem, smem, vmem, vmem, vmem, vmem],
        out_specs=vmem,
        scratch_shapes=[
            pltpu.VMEM((2 * N_COL, RBS, RBS), BF16),
            pltpu.VMEM((NG * CAP, RBS, 2 * RBS), BF16),
            pltpu.VMEM((NG * CAP, RBS, 2 * RBS), BF16),
            pltpu.VMEM((NA * 2 * BLK, RBS, RBS), BF16),
            pltpu.VMEM((NG, CAP, RBS // NA, RBS), BF16),
            pltpu.VMEM((NA * NG, CAP, RBS // NA, RBS), BF16),
            pltpu.VMEM((NA * 2 * BLK, RBS, RBS), BF16),
            pltpu.VMEM((NG, 2 * RBS, CAP * RBS), BF16),
            pltpu.VMEM((RBS, RBS), BF16),
        ]
        + [pltpu.VMEM((TILES + 1, RBS, RBS), BF16)] * NG
        + [
            dma((NG * CAP,)),
            dma((NG * CAP,)),
            dma((NG,)),
            dma((NG,)),
            dma((9,)),
            dma((9,)),
            dma((80,)),
            dma((80,)),
        ],
        compiler_params=pltpu.CompilerParams(
            collective_id=0, has_side_effects=True, vmem_limit_bytes=56 << 20
        ),
    )(tab, keep, colloc, potent, weights, density)


def solution(mesh):
    placed = (
        P("grid", None, "ao"),
        P("grid", None, "ao"),
        P("grid", None),
        P("grid", None),
        P(),
        P(),
    )
    return jax.shard_map(
        local, mesh=mesh, in_specs=placed, out_specs=P("grid", "ao"), check_vma=False
    )
```

```python
import functools

import jax
import jax.numpy as jnp
from jax import lax
from jax.experimental import pallas as pl
from jax.experimental.pallas import tpu as pltpu
from jax.sharding import PartitionSpec as P

RBS = 128
SIG = 8
BLK = 4
NG = 32
NA = 4
NY = 4
NX = 4
CAP = 2
TILES = 16
N_COL = 64
MESH = pl.DeviceIdType.MESH
F32 = jnp.float32
BF16 = jnp.bfloat16

T_K0 = 0
T_K1 = T_K0 + NG * CAP
T_ARR = T_K1 + NG * CAP
T_CB = T_ARR + BLK * SIG
T_SEL = T_CB + NG * CAP
T_IDX = T_SEL + TILES
T_END = T_IDX + NG * CAP * TILES

OFFSETS = sorted(
    [(oy, ox, oc) for oy in range(NY) for ox in range(NX) for oc in range(2) if (oy, ox, oc) != (0, 0, 0)],
    key=lambda o: -(min(o[0], NY - o[0]) + min(o[1], NX - o[1])),
)


def plan(list_owner, list_local, me, part):
    owners = list_owner.reshape(NG, BLK, SIG)
    local_rows = list_local.reshape(NG, BLK, SIG)
    row_ids = owners * 2 + local_rows
    i32 = jnp.int32
    places = jnp.arange(CAP, dtype=i32)
    lower = (jnp.arange(BLK)[:, None] > jnp.arange(BLK)[None, :]).astype(i32)

    hit = (owners == me).astype(i32)
    named = jnp.sum(hit, axis=2)
    before = jnp.sum(named[:, None, :] * lower[None], axis=2)
    chosen = named[:, None, :] * (before[:, None, :] == places[None, :, None]).astype(i32)
    valid = jnp.sum(chosen, axis=2)
    row = jnp.sum(chosen * jnp.sum(hit * local_rows, axis=2)[:, None, :], axis=2)
    my_cols = lax.dynamic_slice_in_dim(row_ids, part * 2, 2, axis=2)
    cols = jnp.sum(chosen[:, :, :, None] * my_cols[:, None], axis=2)
    keep = (valid[:, :, None] * (row[:, :, None] == jnp.arange(2, dtype=i32))).astype(F32)

    mine = lax.dynamic_index_in_dim(owners, me, 0, keepdims=False)
    mine_named = jnp.sum((mine[:, :, None] == jnp.arange(NG, dtype=i32)).astype(i32), axis=1)
    mine_before = jnp.sum(mine_named[None] * lower[:, :, None], axis=1)
    same = (mine[:, :, None] == jnp.arange(NG, dtype=i32)).astype(i32)
    spot = jnp.sum(same * mine_before[:, None, :], axis=2)
    arr = mine * CAP + spot

    pick = mine_named[None] * (mine_before[None] == places[:, None, None]).astype(i32)
    cb = jnp.sum(pick * jnp.arange(BLK, dtype=i32)[None, :, None], axis=1)
    slot = jnp.sum(same * jnp.arange(SIG, dtype=i32)[None, :, None], axis=1)
    cj = jnp.sum(pick * slot[None], axis=1)
    cb = (cj // 2) * (2 * BLK) + cb * 2 + cj % 2

    group = (owners // (NG // NA) == part).astype(i32).reshape(NG, BLK * SIG)
    n = BLK * SIG
    below = (jnp.arange(n)[:, None] > jnp.arange(n)[None, :]).astype(i32)
    rank = jnp.sum(group[:, None, :] * below[None], axis=2)
    my_group = lax.dynamic_index_in_dim(group, me, 0, keepdims=False)
    my_rank = lax.dynamic_index_in_dim(rank, me, 0, keepdims=False)
    flat = jnp.arange(n, dtype=i32)
    b_of, k_of = flat // SIG, flat % SIG
    stored = (k_of // 2) * (2 * BLK) + (k_of % 2) * BLK + b_of
    tiles = jnp.arange(TILES, dtype=i32)
    sel = jnp.sum(my_group[None] * (my_rank[None] == tiles[:, None]).astype(i32) * stored[None], axis=1)

    here = (row_ids[:, :, :, None] == part * TILES + tiles).astype(i32)
    at = jnp.sum(here * (rank.reshape(NG, BLK, SIG)[..., None] - TILES), axis=2)
    idx = TILES + jnp.sum(chosen[..., None] * at[:, None], axis=2)

    tab = jnp.concatenate(
        [
            (row * N_COL + cols[:, :, 0]).reshape(-1),
            (row * N_COL + cols[:, :, 1]).reshape(-1),
            arr.reshape(-1),
            cb.T.reshape(-1),
            sel,
            idx.reshape(-1),
        ]
    )
    return tab, keep.reshape(-1)


def kernel(tab, keep, colloc, potent, weights, dens, out, dtiles, send0, send1, arrived0, arrived1, cfull, cqs, cown, wz, lhs_t, picked, scaled, *rest):
    held = rest[: NG]
    dsend, drecv, csend, crecv, zsend, zrecv, gsend, grecv = rest[NG:]
    me = lax.axis_index("grid")
    part = lax.axis_index("ao")
    y = me // (2 * NX)
    x = (me // 2) % NX
    core = me % 2

    def at_offset(oy, ox, oc):
        return ((y + oy + NY) % NY) * (2 * NX) + ((x + ox + NX) % NX) * 2 + (core + oc) % 2

    barrier = pltpu.get_barrier_semaphore()
    for o in OFFSETS:
        pl.semaphore_signal(barrier, inc=1, device_id=(at_offset(*o), part), device_id_type=MESH)
    for o in range(1, NA):
        pl.semaphore_signal(barrier, inc=1, device_id=(me, (part + o) % NA), device_id_type=MESH)

    send = (send0, send1)
    arrived = (arrived0, arrived1)

    def pack(h):
        def step(d, carry):
            for c in range(CAP):
                send[h][d * CAP + c] = dtiles[tab[(T_K0, T_K1)[h] + d * CAP + c]]
            return carry

        lax.fori_loop(0, NG, step, 0)

    for r in range(2):
        for k in range(N_COL):
            dtiles[r * N_COL + k] = dens[r * RBS : (r + 1) * RBS, k * RBS : (k + 1) * RBS]
    pack(0)
    for b in range(BLK):
        for h in range(2):
            cfull[part * 2 * BLK + 2 * b + h] = colloc[b, :, h * RBS : (h + 1) * RBS]
    pl.semaphore_wait(barrier, len(OFFSETS) + NA - 1)

    def z_copy(buf, base, o, there, cut=(0, 1)):
        whole = buf.shape[0] // NA
        count = whole // cut[1]
        low = cut[0] * count
        return pltpu.make_async_remote_copy(
            src_ref=buf.at[pl.ds(part * whole + low, count)],
            dst_ref=buf.at[pl.ds(there * whole + low, count)],
            send_sem=zsend.at[base + o - 1],
            recv_sem=zrecv.at[base + o - 1],
            device_id=(me, (part + o) % NA),
            device_id_type=MESH,
        )

    def z_start(buf, base, cut=(0, 1)):
        for o in (2, 1, 3):
            z_copy(buf, base, o, part, cut).start()

    def z_wait_recv(buf, base, cut=(0, 1)):
        for o in (1, 3, 2):
            z_copy(buf, base, o, (part + NA - o) % NA, cut).wait_recv()

    def z_wait_send(buf, base, cut=(0, 1)):
        for o in (1, 2, 3):
            z_copy(buf, base, o, part, cut).wait_send()

    def d_copy(n, h, recv):
        oy, ox, oc = OFFSETS[n]
        to = at_offset(oy, ox, oc)
        frm = at_offset(-oy, -ox, oc) if recv else me
        return pltpu.make_async_remote_copy(
            src_ref=send[h].at[pl.ds(to * CAP, CAP)],
            dst_ref=arrived[h].at[pl.ds(frm * CAP, CAP)],
            send_sem=dsend.at[n * 2 + h],
            recv_sem=drecv.at[n * 2 + h],
            device_id=(to, part),
            device_id_type=MESH,
        )

    def c_copy(n, recv):
        oy, ox, oc = OFFSETS[n]
        to = at_offset(oy, ox, oc)
        frm = at_offset(-oy, -ox, oc) if recv else me
        return pltpu.make_async_remote_copy(
            src_ref=cqs.at[to],
            dst_ref=cown.at[part * NG + frm],
            send_sem=csend.at[n],
            recv_sem=crecv.at[n],
            device_id=(to, part),
            device_id_type=MESH,
        )

    z_start(cfull, 0)
    for n in range(NG - 1):
        d_copy(n, 0, False).start()
    pack(1)
    for n in range(NG - 1):
        d_copy(n, 1, False).start()
    for h in range(2):
        for c in range(CAP):
            arrived[h][me * CAP + c] = send[h][me * CAP + c]
    for b in range(BLK):
        w = jnp.transpose(jnp.broadcast_to(weights[b : b + 1, :], (RBS, RBS)))
        for h in range(2):
            scaled[h * BLK + b] = w * potent[b, :, h * RBS : (h + 1) * RBS].astype(F32)
    for s in range(NG):
        held[s][TILES] = jnp.zeros((RBS, RBS), BF16)
    out[...] = jnp.zeros_like(out)

    z_wait_recv(cfull, 0)
    quarter = RBS // NA

    def pack_c(o, carry):
        for c in range(CAP):
            picked[...] = cfull[tab[T_CB + o * CAP + c]]
            rows = pl.multiple_of(part * quarter, quarter)
            cqs[o, c] = picked[pl.ds(rows, quarter), :]
        return carry

    lax.fori_loop(0, NG, pack_c, 0)
    for n in range(NG - 1):
        c_copy(n, False).start()
    cown[part * NG + me] = cqs[me]

    for h in range(2):
        for n in range(NG - 1):
            d_copy(n, h, True).wait_recv()
        for b in range(BLK):
            left = jnp.concatenate([cfull[q * 2 * BLK + 2 * b + g] for q in range(NA) for g in range(2)], axis=1)
            right = jnp.concatenate([arrived[h][tab[T_ARR + b * SIG + j]] for j in range(SIG)], axis=0)
            f_vals = jnp.dot(left, right, preferred_element_type=F32)
            wz[part * 2 * BLK + h * BLK + b] = (scaled[h * BLK + b] * f_vals).astype(BF16)
        z_start(wz, 3 + 3 * h, (h, 2))
    for n in range(NG - 1):
        c_copy(n, True).wait_recv()
    z_start(cown, 9)
    for h in range(2):
        z_wait_recv(wz, 3 + 3 * h, (h, 2))

    def build(d, carry):
        for c in range(CAP):
            tile = jnp.concatenate([cown[q * NG + d, c].astype(F32) for q in range(NA)], axis=0)
            tile = jnp.transpose(tile)
            for r in range(2):
                lhs_t[d, r * RBS : (r + 1) * RBS, c * RBS : (c + 1) * RBS] = (
                    tile * keep[(d * CAP + c) * 2 + r]
                ).astype(BF16)
        return carry

    def piece(oy, ox, oc=0):
        return held[((oy % NY) * NX + ox % NX) * 2 + oc]

    own = piece(0, 0)
    for t in range(TILES):
        own[t] = wz[tab[T_SEL + t]]

    moves = {}

    def move(key, oy, ox, low, count, dy, dx, dc=0):
        n = len(moves)
        rows = pl.ds(low, count)
        copy = pltpu.make_async_remote_copy(
            src_ref=piece(oy, ox).at[rows],
            dst_ref=piece(oy + dy, ox + dx, dc).at[rows],
            send_sem=gsend.at[n],
            recv_sem=grecv.at[n],
            device_id=(at_offset(dy, dx, dc), part),
            device_id_type=MESH,
        )
        moves[key] = copy
        copy.start()

    first = ((0, 1), (1, 0))
    second = ((1, 0), (0, 1))
    half = TILES // 2

    def along(h, i, s=0):
        (py, px), (qy, qx) = first[h], second[h]
        return (i * py + s * qy, i * px + s * qx)

    def send_first(h):
        for s in (1, -1):
            move(("p", h, s), 0, 0, h * half, half, *along(h, s))

    def send_second(h, i):
        for s in (1, -1):
            move(("q", h, i, s), *along(h, i), h * half, half, *along(h, 0, s))

    def split(h, s):
        return h * half + (0 if s > 0 else half // 2), half // 2

    def forward_first(h, s):
        moves["p", h, s].wait_recv()
        move(("pf", h, s), *along(h, s), *split(h, s), *along(h, s))

    def forward_second(h, i, s):
        moves["q", h, i, s].wait_recv()
        move(("qf", h, i, s), *along(h, i, s), *split(h, s), *along(h, 0, s))

    def to_sibling(oy, ox):
        move(("s", oy % NY, ox % NX), oy, ox, 0, TILES, 0, 0, 1)

    def add_piece(oy, ox, oc):
        src = at_offset(-oy, -ox, oc)
        buf = piece(oy, ox, oc)
        tiles = []
        for c in range(CAP):
            base = T_IDX + (src * CAP + c) * TILES
            tiles.append(jnp.concatenate([buf[tab[base + w]] for w in range(TILES)], axis=1))
        out[...] += jnp.dot(lhs_t[src], jnp.concatenate(tiles, axis=0), preferred_element_type=F32)

    def finish(pieces):
        for oy, ox in pieces:
            to_sibling(oy, ox)

    def add(pieces, oc):
        for oy, ox in pieces:
            if oc:
                moves["s", oy % NY, ox % NX].wait_recv()
            add_piece(oy, ox, oc)

    for h in range(2):
        send_first(h)
    for h in range(2):
        send_second(h, 0)
    to_sibling(0, 0)
    for s in (1, -1):
        for h in range(2):
            forward_first(h, s)
            send_second(h, s)
    for s in (1, -1):
        for h in range(2):
            forward_second(h, 0, s)
    near = [(0, 1), (0, -1), (1, 0), (-1, 0)]
    finish(near)
    for h in range(2):
        for s in (1, -1):
            moves["pf", h, s].wait_recv()
        send_second(h, 2)
    diagonal = [(1, 1), (1, -1), (-1, 1), (-1, -1)]
    for i in (1, -1):
        for s in (1, -1):
            for h in range(2):
                forward_second(h, i, s)
    finish(diagonal)
    for h in range(2):
        for s in (1, -1):
            moves["qf", h, 0, s].wait_recv()
    straight = [(0, 2), (2, 0)]
    finish(straight)
    for s in (1, -1):
        for h in range(2):
            forward_second(h, 2, s)
    z_wait_recv(cown, 9)
    lax.fori_loop(0, NG, build, 0)
    for pieces in ([(0, 0)], near, diagonal, straight):
        add(pieces, 0)
        add(pieces, 1)
    for i in (1, -1):
        for h in range(2):
            for s in (1, -1):
                moves["qf", h, i, s].wait_recv()
    knight = [(1, 2), (-1, 2), (2, 1), (2, -1)]
    finish(knight)
    add(knight, 0)
    for h in range(2):
        for s in (1, -1):
            moves["qf", h, 2, s].wait_recv()
    last = [(2, 2)]
    finish(last)
    add(knight, 1)
    add(last, 0)
    add(last, 1)

    for n in range(NG - 1):
        for h in range(2):
            d_copy(n, h, False).wait_send()
        c_copy(n, False).wait_send()
    z_wait_send(cfull, 0)
    for h in range(2):
        z_wait_send(wz, 3 + 3 * h, (h, 2))
    z_wait_send(cown, 9)
    for copy in moves.values():
        copy.wait_send()


def local(colloc, potent, weights, density, list_owner, list_local):
    me = lax.axis_index("grid")
    part = lax.axis_index("ao")
    tab, keep = plan(list_owner, list_local, me, part)
    smem = pl.BlockSpec(memory_space=pltpu.SMEM)
    vmem = pl.BlockSpec(memory_space=pltpu.VMEM)
    dma = pltpu.SemaphoreType.DMA
    return pl.pallas_call(
        kernel,
        out_shape=jax.ShapeDtypeStruct((2 * RBS, TILES * RBS), F32),
        in_specs=[smem, smem, vmem, vmem, vmem, vmem],
        out_specs=vmem,
        scratch_shapes=[
            pltpu.VMEM((2 * N_COL, RBS, RBS), BF16),
            pltpu.VMEM((NG * CAP, RBS, RBS), BF16),
            pltpu.VMEM((NG * CAP, RBS, RBS), BF16),
            pltpu.VMEM((NG * CAP, RBS, RBS), BF16),
            pltpu.VMEM((NG * CAP, RBS, RBS), BF16),
            pltpu.VMEM((NA * 2 * BLK, RBS, RBS), BF16),
            pltpu.VMEM((NG, CAP, RBS // NA, RBS), BF16),
            pltpu.VMEM((NA * NG, CAP, RBS // NA, RBS), BF16),
            pltpu.VMEM((NA * 2 * BLK, RBS, RBS), BF16),
            pltpu.VMEM((NG, 2 * RBS, CAP * RBS), BF16),
            pltpu.VMEM((RBS, RBS), BF16),
            pltpu.VMEM((2 * BLK, RBS, RBS), F32),
        ]
        + [pltpu.VMEM((TILES + 1, RBS, RBS), BF16)] * NG
        + [
            dma((NG * 2,)),
            dma((NG * 2,)),
            dma((NG,)),
            dma((NG,)),
            dma((12,)),
            dma((12,)),
            dma((80,)),
            dma((80,)),
        ],
        compiler_params=pltpu.CompilerParams(
            collective_id=0, has_side_effects=True, vmem_limit_bytes=56 << 20
        ),
    )(tab, keep, colloc, potent, weights, density)


def solution(mesh):
    placed = (
        P("grid", None, "ao"),
        P("grid", None, "ao"),
        P("grid", None),
        P("grid", None),
        P(),
        P(),
    )
    return jax.shard_map(
        local, mesh=mesh, in_specs=placed, out_specs=P("grid", "ao"), check_vma=False
    )
```

```python
import functools

import jax
import jax.numpy as jnp
from jax import lax
from jax.experimental import pallas as pl
from jax.experimental.pallas import tpu as pltpu
from jax.sharding import PartitionSpec as P

RBS = 128
SIG = 8
BLK = 4
NG = 32
NA = 4
NY = 4
NX = 4
CAP = 2
TILES = 16
FEW = 13
N_COL = 64
MESH = pl.DeviceIdType.MESH
F32 = jnp.float32
BF16 = jnp.bfloat16

LANES = 128
T_ARR = 0
T_DENS = T_ARR + SIG
T_CB = T_DENS + 2 * CAP
T_SEL = T_CB + 1
T_IDX = 16
T_END = T_IDX + CAP * TILES


def exchange_order():
    far = sorted(
        [(oy, ox, oc) for oy in range(NY) for ox in range(NX) for oc in range(2) if (oy, ox, oc) != (0, 0, 0)],
        key=lambda o: -(min(o[0], NY - o[0]) + min(o[1], NX - o[1])),
    )
    order = []
    for first in far:
        turned = first
        for _ in range(4):
            if turned not in order:
                order.append(turned)
            turned = (turned[1] % NY, -turned[0] % NX, turned[2])
    return order


OFFSETS = exchange_order()


def plan_kernel(own_ref, loc_ref, tab, keep, few):
    me = lax.axis_index("grid")
    part = lax.axis_index("ao")
    i32 = jnp.int32
    own = own_ref[...]
    loc = loc_ref[...]
    shape = (SIG, LANES)
    slot = lax.broadcasted_iota(i32, shape, 0)
    lane = lax.broadcasted_iota(i32, shape, 1)
    block = lane % BLK
    row1 = (1, LANES)
    block1 = lax.broadcasted_iota(i32, row1, 1) % BLK
    row_ids = own * 2 + loc

    def total(v):
        return jnp.sum(v, axis=0, keepdims=True)

    def earlier(v, blk):
        out = jnp.zeros_like(v)
        for s in range(1, BLK):
            out += jnp.where(blk >= s, pltpu.roll(v, s, 1), 0)
        return out

    def over_blocks(v):
        out = v
        for s in range(1, BLK):
            out += pltpu.roll(v, LANES - s, 1)
        return out

    hit = (own == me).astype(i32)
    named = total(hit)
    before = earlier(named, block1)
    row = total(hit * loc)
    cols = [total(jnp.where(slot == part * 2 + h, row_ids, 0)) for h in range(2)]
    chosen = [named * (before == c).astype(i32) for c in range(CAP)]
    for c in range(CAP):
        for h in range(2):
            tab[T_DENS + h * CAP + c, :] = over_blocks(chosen[c] * (row * N_COL + cols[h]))[0]
        for r in range(2):
            keep[c * 2 + r, :] = over_blocks(chosen[c] * (row == r).astype(i32))[0].astype(F32)

    spot = jnp.zeros(shape, i32)
    for s in range(1, BLK):
        prior = pltpu.roll(own, s, 1)
        for j in range(SIG):
            turned = prior if j == 0 else pltpu.roll(prior, j, 0)
            spot += jnp.where((block >= s) & (turned == own), 1, 0)
    arr = own * CAP + spot
    tab[T_ARR : T_ARR + SIG, :] = arr

    group = (own // (NG // NA) == part).astype(i32)
    rank = earlier(total(group), block1) + jnp.zeros(shape, i32)
    for s in range(1, SIG):
        rank += jnp.where(slot >= s, pltpu.roll(group, s, 0), 0)
    to_me = LANES - me * BLK
    my_arr = pltpu.roll(arr, to_me, 1)
    my_rank = pltpu.roll(jnp.where(group > 0, rank, LANES), to_me, 1)
    cb = jnp.zeros(row1, i32)
    sel = jnp.zeros(row1, i32)
    for b in range(BLK):
        at = (slot // 2) * (2 * BLK) + 2 * b + slot % 2
        cb += total(jnp.where(jnp.broadcast_to(my_arr[:, b : b + 1], shape) == lane, at, 0))
        at = (slot // 2) * (2 * BLK) + (slot % 2) * BLK + b
        sel += total(jnp.where(jnp.broadcast_to(my_rank[:, b : b + 1], shape) == lane, at, 0))
    tab[T_CB, :] = cb[0]
    tab[T_SEL, :] = sel[0]
    for n in range(TILES):
        at = total(jnp.where(row_ids == part * TILES + n, rank + 1, 0))
        for c in range(CAP):
            tab[T_IDX + c * TILES + n, :] = over_blocks(chosen[c] * at)[0]

    most = jnp.zeros(row1, i32)
    for z in range(NA):
        most = jnp.maximum(most, over_blocks(total((own // (NG // NA) == z).astype(i32))))
    most = jnp.where(block1 == 0, most, 0)
    few[0, 0] = (jnp.max(most) <= FEW).astype(i32)


def kernel(count, tab, keep, colloc, potent, weights, dens, out, dtiles, send0, send1, arrived0, arrived1, cfull, cqs, cown, wz, lhs_t, picked, scaled, dloc, *rest):
    held = rest[: NG]
    dsend, drecv, csend, crecv, zsend, zrecv, gsend, grecv, lsem = rest[NG:]
    me = lax.axis_index("grid")
    part = lax.axis_index("ao")
    y = me // (2 * NX)
    x = (me // 2) % NX
    core = me % 2

    def at_offset(oy, ox, oc):
        return ((y + oy + NY) % NY) * (2 * NX) + ((x + ox + NX) % NX) * 2 + (core + oc) % 2

    rows_in = [
        pltpu.make_async_copy(dens.at[pl.ds(r * RBS, RBS)], dloc.at[pl.ds(r * RBS, RBS)], lsem.at[r]) for r in range(2)
    ]
    for copy in rows_in:
        copy.start()
    barrier = pltpu.get_barrier_semaphore()
    for o in OFFSETS:
        pl.semaphore_signal(barrier, inc=1, device_id=(at_offset(*o), part), device_id_type=MESH)
    for o in range(1, NA):
        pl.semaphore_signal(barrier, inc=1, device_id=(me, (part + o) % NA), device_id_type=MESH)

    send = (send0, send1)
    arrived = (arrived0, arrived1)

    def pack(h):
        def step(d, carry):
            for c in range(CAP):
                send[h][d * CAP + c] = dtiles[tab[T_DENS + h * CAP + c, d * BLK]]
            return carry

        lax.fori_loop(0, NG, step, 0)

    for r in range(2):
        rows_in[r].wait()
        for k in range(N_COL):
            dtiles[r * N_COL + k] = dloc[r * RBS : (r + 1) * RBS, k * RBS : (k + 1) * RBS]
    pack(0)
    for b in range(BLK):
        for h in range(2):
            cfull[part * 2 * BLK + 2 * b + h] = colloc[b, :, h * RBS : (h + 1) * RBS]
    pl.semaphore_wait(barrier, len(OFFSETS) + NA - 1)

    def z_copy(buf, base, o, there, cut=(0, 1)):
        whole = buf.shape[0] // NA
        count = whole // cut[1]
        low = cut[0] * count
        return pltpu.make_async_remote_copy(
            src_ref=buf.at[pl.ds(part * whole + low, count)],
            dst_ref=buf.at[pl.ds(there * whole + low, count)],
            send_sem=zsend.at[base + o - 1],
            recv_sem=zrecv.at[base + o - 1],
            device_id=(me, (part + o) % NA),
            device_id_type=MESH,
        )

    def z_start(buf, base, cut=(0, 1)):
        for o in (2, 1, 3):
            z_copy(buf, base, o, part, cut).start()

    def z_wait_recv(buf, base, cut=(0, 1)):
        for o in (1, 3, 2):
            z_copy(buf, base, o, (part + NA - o) % NA, cut).wait_recv()

    def z_wait_send(buf, base, cut=(0, 1)):
        for o in (1, 2, 3):
            z_copy(buf, base, o, part, cut).wait_send()

    def d_copy(n, h, recv):
        oy, ox, oc = OFFSETS[n]
        to = at_offset(oy, ox, oc)
        frm = at_offset(-oy, -ox, oc) if recv else me
        return pltpu.make_async_remote_copy(
            src_ref=send[h].at[pl.ds(to * CAP, CAP)],
            dst_ref=arrived[h].at[pl.ds(frm * CAP, CAP)],
            send_sem=dsend.at[n * 2 + h],
            recv_sem=drecv.at[n * 2 + h],
            device_id=(to, part),
            device_id_type=MESH,
        )

    def c_copy(n, recv):
        oy, ox, oc = OFFSETS[n]
        to = at_offset(oy, ox, oc)
        frm = at_offset(-oy, -ox, oc) if recv else me
        return pltpu.make_async_remote_copy(
            src_ref=cqs.at[to],
            dst_ref=cown.at[part * NG + frm],
            send_sem=csend.at[n],
            recv_sem=crecv.at[n],
            device_id=(to, part),
            device_id_type=MESH,
        )

    z_start(cfull, 0)
    for n in range(NG - 1):
        d_copy(n, 0, False).start()
    pack(1)
    for n in range(NG - 1):
        d_copy(n, 1, False).start()
    for h in range(2):
        for c in range(CAP):
            arrived[h][me * CAP + c] = send[h][me * CAP + c]
    for b in range(BLK):
        w = jnp.transpose(jnp.broadcast_to(weights[b : b + 1, :], (RBS, RBS)))
        for h in range(2):
            scaled[h * BLK + b] = w * potent[b, :, h * RBS : (h + 1) * RBS].astype(F32)
    for s in range(NG):
        held[s][0] = jnp.zeros((RBS, RBS), BF16)
    out[...] = jnp.zeros_like(out)

    z_wait_recv(cfull, 0)
    quarter = RBS // NA

    def pack_c(o, carry):
        for c in range(CAP):
            picked[...] = cfull[tab[T_CB, o * CAP + c]]
            rows = pl.multiple_of(part * quarter, quarter)
            cqs[o, c] = picked[pl.ds(rows, quarter), :]
        return carry

    lax.fori_loop(0, NG, pack_c, 0)
    for n in range(NG - 1):
        c_copy(n, False).start()
    cown[part * NG + me] = cqs[me]

    for h in range(2):
        for n in range(NG - 1):
            d_copy(n, h, True).wait_recv()
        for b in range(BLK):
            left = jnp.concatenate([cfull[q * 2 * BLK + 2 * b + g] for q in range(NA) for g in range(2)], axis=1)
            right = jnp.concatenate([arrived[h][tab[T_ARR + j, me * BLK + b]] for j in range(SIG)], axis=0)
            f_vals = jnp.dot(left, right, preferred_element_type=F32)
            wz[part * 2 * BLK + h * BLK + b] = (scaled[h * BLK + b] * f_vals).astype(BF16)
        z_start(wz, 3 + 3 * h, (h, 2))
    for n in range(NG - 1):
        c_copy(n, True).wait_recv()
    z_start(cown, 9)
    for h in range(2):
        z_wait_recv(wz, 3 + 3 * h, (h, 2))

    def build(d, carry):
        for c in range(CAP):
            tile = jnp.concatenate([cown[q * NG + d, c].astype(F32) for q in range(NA)], axis=0)
            tile = jnp.transpose(tile)
            for r in range(2):
                lhs_t[d, r * RBS : (r + 1) * RBS, c * RBS : (c + 1) * RBS] = (
                    tile * keep[c * 2 + r, d * BLK]
                ).astype(BF16)
        return carry

    def piece(oy, ox, oc=0):
        return held[((oy % NY) * NX + ox % NX) * 2 + oc]

    own = piece(0, 0)
    for t in range(count):
        own[1 + t] = wz[tab[T_SEL, t]]

    moves = {}

    def move(key, oy, ox, low, size, dy, dx, dc=0):
        n = len(moves)
        rows = pl.ds(1 + low, size)
        copy = pltpu.make_async_remote_copy(
            src_ref=piece(oy, ox).at[rows],
            dst_ref=piece(oy + dy, ox + dx, dc).at[rows],
            send_sem=gsend.at[n],
            recv_sem=grecv.at[n],
            device_id=(at_offset(dy, dx, dc), part),
            device_id_type=MESH,
        )
        moves[key] = copy
        copy.start()

    first = ((0, 1), (1, 0))
    second = ((1, 0), (0, 1))
    sizes = (count - count // 2, count // 2)
    lows = (0, sizes[0])

    def along(h, i, s=0):
        (py, px), (qy, qx) = first[h], second[h]
        return (i * py + s * qy, i * px + s * qx)

    def send_first(h):
        for s in (1, -1):
            move(("p", h, s), 0, 0, lows[h], sizes[h], *along(h, s))

    def send_second(h, i):
        for s in (1, -1):
            move(("q", h, i, s), *along(h, i), lows[h], sizes[h], *along(h, 0, s))

    def split(h, s):
        near_half = sizes[h] // 2 if h else sizes[h] - sizes[h] // 2
        return (lows[h], near_half) if s > 0 else (lows[h] + near_half, sizes[h] - near_half)

    def forward_first(h, s):
        moves["p", h, s].wait_recv()
        move(("pf", h, s), *along(h, s), *split(h, s), *along(h, s))

    def forward_second(h, i, s):
        moves["q", h, i, s].wait_recv()
        move(("qf", h, i, s), *along(h, i, s), *split(h, s), *along(h, 0, s))

    def to_sibling(oy, ox):
        move(("s", oy % NY, ox % NX), oy, ox, 0, count, 0, 0, 1)

    def add_piece(oy, ox, oc):
        src = at_offset(-oy, -ox, oc)
        buf = piece(oy, ox, oc)
        tiles = []
        for c in range(CAP):
            base = T_IDX + c * TILES
            tiles.append(jnp.concatenate([buf[tab[base + w, src * BLK]] for w in range(TILES)], axis=1))
        out[...] += jnp.dot(lhs_t[src], jnp.concatenate(tiles, axis=0), preferred_element_type=F32)

    def finish(pieces):
        for oy, ox in pieces:
            to_sibling(oy, ox)

    def add(pieces, oc):
        for oy, ox in pieces:
            if oc:
                moves["s", oy % NY, ox % NX].wait_recv()
            add_piece(oy, ox, oc)

    for h in range(2):
        send_first(h)
    for h in range(2):
        send_second(h, 0)
    to_sibling(0, 0)
    for s in (1, -1):
        for h in range(2):
            forward_first(h, s)
            send_second(h, s)
    for s in (1, -1):
        for h in range(2):
            forward_second(h, 0, s)
    near = [(0, 1), (0, -1), (1, 0), (-1, 0)]
    finish(near)
    for h in range(2):
        for s in (1, -1):
            moves["pf", h, s].wait_recv()
        send_second(h, 2)
    diagonal = [(1, 1), (1, -1), (-1, 1), (-1, -1)]
    for i in (1, -1):
        for s in (1, -1):
            for h in range(2):
                forward_second(h, i, s)
    finish(diagonal)
    for h in range(2):
        for s in (1, -1):
            moves["qf", h, 0, s].wait_recv()
    straight = [(0, 2), (2, 0)]
    finish(straight)
    for s in (1, -1):
        for h in range(2):
            forward_second(h, 2, s)
    z_wait_recv(cown, 9)
    lax.fori_loop(0, NG, build, 0)
    for pieces in ([(0, 0)], near, diagonal, straight):
        add(pieces, 0)
        add(pieces, 1)
    for i in (1, -1):
        for h in range(2):
            for s in (1, -1):
                moves["qf", h, i, s].wait_recv()
    knight = [(1, 2), (-1, 2), (2, 1), (2, -1)]
    finish(knight)
    for n in range(NG - 1):
        for h in range(2):
            d_copy(n, h, False).wait_send()
        c_copy(n, False).wait_send()
    z_wait_send(cfull, 0)
    for h in range(2):
        z_wait_send(wz, 3 + 3 * h, (h, 2))
    z_wait_send(cown, 9)
    add(knight, 0)
    add(knight, 1)
    earlier = list(moves.values())
    for h in range(2):
        for s in (1, -1):
            moves["qf", h, 2, s].wait_recv()
        move(("s2", h), 2, 2, lows[h], sizes[h], 0, 0, 1)
    add_piece(2, 2, 0)
    for copy in earlier:
        copy.wait_send()
    for h in range(2):
        moves["s2", h].wait_recv()
    add_piece(2, 2, 1)
    for h in range(2):
        moves["s2", h].wait_send()


def local(colloc, potent, weights, density, list_owner, list_local):
    smem = pl.BlockSpec(memory_space=pltpu.SMEM)
    vmem = pl.BlockSpec(memory_space=pltpu.VMEM)
    tab, keep, few = pl.pallas_call(
        plan_kernel,
        out_shape=(
            jax.ShapeDtypeStruct((T_END, LANES), jnp.int32),
            jax.ShapeDtypeStruct((2 * CAP, LANES), F32),
            jax.ShapeDtypeStruct((1, 1), jnp.int32),
        ),
        in_specs=[vmem, vmem],
        out_specs=(vmem, vmem, smem),
    )(list_owner.T, list_local.T)
    dma = pltpu.SemaphoreType.DMA
    def exchange(count, collective_id):
        return pl.pallas_call(
            functools.partial(kernel, count),
            out_shape=pltpu.VMEM((2 * RBS, TILES * RBS), F32),
            in_specs=[smem, smem, vmem, vmem, vmem, pl.BlockSpec(memory_space=pl.ANY)],
            out_specs=vmem,
            scratch_shapes=[
                pltpu.VMEM((2 * N_COL, RBS, RBS), BF16),
                pltpu.VMEM((NG * CAP, RBS, RBS), BF16),
                pltpu.VMEM((NG * CAP, RBS, RBS), BF16),
                pltpu.VMEM((NG * CAP, RBS, RBS), BF16),
                pltpu.VMEM((NG * CAP, RBS, RBS), BF16),
                pltpu.VMEM((NA * 2 * BLK, RBS, RBS), BF16),
                pltpu.VMEM((NG, CAP, RBS // NA, RBS), BF16),
                pltpu.VMEM((NA * NG, CAP, RBS // NA, RBS), BF16),
                pltpu.VMEM((NA * 2 * BLK, RBS, RBS), BF16),
                pltpu.VMEM((NG, 2 * RBS, CAP * RBS), BF16),
                pltpu.VMEM((RBS, RBS), BF16),
                pltpu.VMEM((2 * BLK, RBS, RBS), F32),
                pltpu.VMEM((2 * RBS, N_COL * RBS), BF16),
            ]
            + [pltpu.VMEM((count + 1, RBS, RBS), BF16)] * NG
            + [
                dma((NG * 2,)),
                dma((NG * 2,)),
                dma((NG,)),
                dma((NG,)),
                dma((12,)),
                dma((12,)),
                dma((80,)),
                dma((80,)),
                dma((2,)),
            ],
            compiler_params=pltpu.CompilerParams(
                collective_id=collective_id, has_side_effects=True, vmem_limit_bytes=56 << 20
            ),
        )

    return lax.cond(
        few[0, 0] > 0,
        exchange(FEW, 0),
        exchange(TILES, 1),
        tab, keep, colloc, potent, weights, density,
    )


def solution(mesh):
    placed = (
        P("grid", None, "ao"),
        P("grid", None, "ao"),
        P("grid", None),
        P("grid", None),
        P(),
        P(),
    )
    return jax.shard_map(
        local, mesh=mesh, in_specs=placed, out_specs=P("grid", "ao"), check_vma=False
    )
```

```python
import functools

import jax
import jax.numpy as jnp
from jax import lax
from jax.experimental import pallas as pl
from jax.experimental.pallas import tpu as pltpu
from jax.sharding import PartitionSpec as P

RBS = 128
SIG = 8
BLK = 4
NG = 32
NA = 4
NY = 4
NX = 4
CAP = 2
TILES = 16
FEW = 13
N_COL = 64
MESH = pl.DeviceIdType.MESH
F32 = jnp.float32
BF16 = jnp.bfloat16

LANES = 128
T_ARR = 0
T_DENS = T_ARR + SIG
T_CB = T_DENS + 2 * CAP
T_SEL = T_CB + 1
T_IDX = 16
T_END = T_IDX + CAP * TILES


def exchange_order():
    far = sorted(
        [(oy, ox, oc) for oy in range(NY) for ox in range(NX) for oc in range(2) if (oy, ox, oc) != (0, 0, 0)],
        key=lambda o: -(min(o[0], NY - o[0]) + min(o[1], NX - o[1])),
    )
    order = []
    for first in far:
        turned = first
        for _ in range(4):
            if turned not in order:
                order.append(turned)
            turned = (turned[1] % NY, -turned[0] % NX, turned[2])
    return order


OFFSETS = exchange_order()


def plan_kernel(own_ref, loc_ref, tab, keep, few):
    me = lax.axis_index("grid")
    part = lax.axis_index("ao")
    i32 = jnp.int32
    own = own_ref[...]
    loc = loc_ref[...]
    shape = (SIG, LANES)
    slot = lax.broadcasted_iota(i32, shape, 0)
    lane = lax.broadcasted_iota(i32, shape, 1)
    block = lane % BLK
    row1 = (1, LANES)
    block1 = lax.broadcasted_iota(i32, row1, 1) % BLK
    row_ids = own * 2 + loc

    def total(v):
        return jnp.sum(v, axis=0, keepdims=True)

    def earlier(v, blk):
        out = jnp.zeros_like(v)
        for s in range(1, BLK):
            out += jnp.where(blk >= s, pltpu.roll(v, s, 1), 0)
        return out

    def over_blocks(v):
        out = v
        for s in range(1, BLK):
            out += pltpu.roll(v, LANES - s, 1)
        return out

    hit = (own == me).astype(i32)
    named = total(hit)
    before = earlier(named, block1)
    row = total(hit * loc)
    cols = [total(jnp.where(slot == part * 2 + h, row_ids, 0)) for h in range(2)]
    chosen = [named * (before == c).astype(i32) for c in range(CAP)]
    for c in range(CAP):
        for h in range(2):
            tab[T_DENS + h * CAP + c, :] = over_blocks(chosen[c] * (row * N_COL + cols[h]))[0]
        for r in range(2):
            keep[c * 2 + r, :] = over_blocks(chosen[c] * (row == r).astype(i32))[0].astype(F32)

    spot = jnp.zeros(shape, i32)
    for s in range(1, BLK):
        prior = pltpu.roll(own, s, 1)
        for j in range(SIG):
            turned = prior if j == 0 else pltpu.roll(prior, j, 0)
            spot += jnp.where((block >= s) & (turned == own), 1, 0)
    arr = own * CAP + spot
    tab[T_ARR : T_ARR + SIG, :] = arr

    group = (own // (NG // NA) == part).astype(i32)
    rank = earlier(total(group), block1) + jnp.zeros(shape, i32)
    for s in range(1, SIG):
        rank += jnp.where(slot >= s, pltpu.roll(group, s, 0), 0)
    to_me = LANES - me * BLK
    my_arr = pltpu.roll(arr, to_me, 1)
    my_rank = pltpu.roll(jnp.where(group > 0, rank, LANES), to_me, 1)
    cb = jnp.zeros(row1, i32)
    sel = jnp.zeros(row1, i32)
    for b in range(BLK):
        at = (slot // 2) * (2 * BLK) + 2 * b + slot % 2
        cb += total(jnp.where(jnp.broadcast_to(my_arr[:, b : b + 1], shape) == lane, at, 0))
        at = (slot // 2) * (2 * BLK) + (slot % 2) * BLK + b
        sel += total(jnp.where(jnp.broadcast_to(my_rank[:, b : b + 1], shape) == lane, at, 0))
    tab[T_CB, :] = cb[0]
    tab[T_SEL, :] = sel[0]
    for n in range(TILES):
        at = total(jnp.where(row_ids == part * TILES + n, rank + 1, 0))
        for c in range(CAP):
            tab[T_IDX + c * TILES + n, :] = over_blocks(chosen[c] * at)[0]

    most = jnp.zeros(row1, i32)
    for z in range(NA):
        most = jnp.maximum(most, over_blocks(total((own // (NG // NA) == z).astype(i32))))
    most = jnp.where(block1 == 0, most, 0)
    few[0, 0] = (jnp.max(most) <= FEW).astype(i32)


def kernel(count, tab, keep, colloc, potent, weights, dens, out, dtiles, send0, send1, arrived0, arrived1, cfull, cqs, cown, wz, lhs_t, picked, scaled, dloc, *rest):
    held = rest[: NG]
    dsend, drecv, csend, crecv, zsend, zrecv, gsend, grecv, lsem = rest[NG:]
    me = lax.axis_index("grid")
    part = lax.axis_index("ao")
    y = me // (2 * NX)
    x = (me // 2) % NX
    core = me % 2

    def at_offset(oy, ox, oc):
        return ((y + oy + NY) % NY) * (2 * NX) + ((x + ox + NX) % NX) * 2 + (core + oc) % 2

    rows_in = [
        pltpu.make_async_copy(dens.at[pl.ds(r * RBS, RBS)], dloc.at[pl.ds(r * RBS, RBS)], lsem.at[r]) for r in range(2)
    ]
    for copy in rows_in:
        copy.start()
    barrier = pltpu.get_barrier_semaphore()
    for o in OFFSETS:
        pl.semaphore_signal(barrier, inc=1, device_id=(at_offset(*o), part), device_id_type=MESH)
    for o in range(1, NA):
        pl.semaphore_signal(barrier, inc=1, device_id=(me, (part + o) % NA), device_id_type=MESH)

    send = (send0, send1)
    arrived = (arrived0, arrived1)

    def pack(h):
        def step(d, carry):
            for c in range(CAP):
                send[h][d * CAP + c] = dtiles[tab[T_DENS + h * CAP + c, d * BLK]]
            return carry

        lax.fori_loop(0, NG, step, 0)

    for r in range(2):
        rows_in[r].wait()
        for k in range(N_COL):
            dtiles[r * N_COL + k] = dloc[r * RBS : (r + 1) * RBS, k * RBS : (k + 1) * RBS]
    pack(0)
    for b in range(BLK):
        for h in range(2):
            cfull[part * 2 * BLK + 2 * b + h] = colloc[b, :, h * RBS : (h + 1) * RBS]
    pl.semaphore_wait(barrier, len(OFFSETS) + NA - 1)

    def z_copy(buf, base, o, there, cut=(0, 1)):
        whole = buf.shape[0] // NA
        count = whole // cut[1]
        low = cut[0] * count
        return pltpu.make_async_remote_copy(
            src_ref=buf.at[pl.ds(part * whole + low, count)],
            dst_ref=buf.at[pl.ds(there * whole + low, count)],
            send_sem=zsend.at[base + o - 1],
            recv_sem=zrecv.at[base + o - 1],
            device_id=(me, (part + o) % NA),
            device_id_type=MESH,
        )

    def z_start(buf, base, cut=(0, 1)):
        for o in (2, 1, 3):
            z_copy(buf, base, o, part, cut).start()

    def z_wait_recv(buf, base, cut=(0, 1)):
        for o in (1, 3, 2):
            z_copy(buf, base, o, (part + NA - o) % NA, cut).wait_recv()

    def z_wait_send(buf, base, cut=(0, 1)):
        for o in (1, 2, 3):
            z_copy(buf, base, o, part, cut).wait_send()

    def d_copy(n, h, recv):
        oy, ox, oc = OFFSETS[n]
        to = at_offset(oy, ox, oc)
        frm = at_offset(-oy, -ox, oc) if recv else me
        return pltpu.make_async_remote_copy(
            src_ref=send[h].at[pl.ds(to * CAP, CAP)],
            dst_ref=arrived[h].at[pl.ds(frm * CAP, CAP)],
            send_sem=dsend.at[n * 2 + h],
            recv_sem=drecv.at[n * 2 + h],
            device_id=(to, part),
            device_id_type=MESH,
        )

    def c_copy(n, recv):
        oy, ox, oc = OFFSETS[n]
        to = at_offset(oy, ox, oc)
        frm = at_offset(-oy, -ox, oc) if recv else me
        return pltpu.make_async_remote_copy(
            src_ref=cqs.at[to],
            dst_ref=cown.at[part * NG + frm],
            send_sem=csend.at[n],
            recv_sem=crecv.at[n],
            device_id=(to, part),
            device_id_type=MESH,
        )

    z_start(cfull, 0)
    for n in range(NG - 1):
        d_copy(n, 0, False).start()
    pack(1)
    for n in range(NG - 1):
        d_copy(n, 1, False).start()
    for h in range(2):
        for c in range(CAP):
            arrived[h][me * CAP + c] = send[h][me * CAP + c]
    for b in range(BLK):
        w = jnp.transpose(jnp.broadcast_to(weights[b : b + 1, :], (RBS, RBS)))
        for h in range(2):
            scaled[h * BLK + b] = w * potent[b, :, h * RBS : (h + 1) * RBS].astype(F32)
    for s in range(NG):
        held[s][0] = jnp.zeros((RBS, RBS), BF16)
    out[...] = jnp.zeros_like(out)

    z_wait_recv(cfull, 0)
    quarter = RBS // NA

    def pack_c(o, carry):
        for c in range(CAP):
            picked[...] = cfull[tab[T_CB, o * CAP + c]]
            rows = pl.multiple_of(part * quarter, quarter)
            cqs[o, c] = picked[pl.ds(rows, quarter), :]
        return carry

    lax.fori_loop(0, NG, pack_c, 0)
    cown[part * NG + me] = cqs[me]

    for h in range(2):
        for n in range(NG - 1):
            d_copy(n, h, True).wait_recv()
        for b in range(BLK):
            left = jnp.concatenate([cfull[q * 2 * BLK + 2 * b + g] for q in range(NA) for g in range(2)], axis=1)
            right = jnp.concatenate([arrived[h][tab[T_ARR + j, me * BLK + b]] for j in range(SIG)], axis=0)
            f_vals = jnp.dot(left, right, preferred_element_type=F32)
            wz[part * 2 * BLK + h * BLK + b] = (scaled[h * BLK + b] * f_vals).astype(BF16)
        z_start(wz, 6 + 3 * h, (h, 2))
    for n in range(NG - 1):
        c_copy(n, False).start()
    for h in range(2):
        z_wait_recv(wz, 6 + 3 * h, (h, 2))

    def build(d, carry):
        for c in range(CAP):
            tile = jnp.concatenate([cown[q * NG + d, c].astype(F32) for q in range(NA)], axis=0)
            tile = jnp.transpose(tile)
            for r in range(2):
                lhs_t[d, r * RBS : (r + 1) * RBS, c * RBS : (c + 1) * RBS] = (
                    tile * keep[c * 2 + r, d * BLK]
                ).astype(BF16)
        return carry

    def piece(oy, ox, oc=0):
        return held[((oy % NY) * NX + ox % NX) * 2 + oc]

    own = piece(0, 0)
    for t in range(count):
        own[1 + t] = wz[tab[T_SEL, t]]

    moves = {}

    def move(key, oy, ox, low, size, dy, dx, dc=0):
        n = len(moves)
        rows = pl.ds(1 + low, size)
        copy = pltpu.make_async_remote_copy(
            src_ref=piece(oy, ox).at[rows],
            dst_ref=piece(oy + dy, ox + dx, dc).at[rows],
            send_sem=gsend.at[n],
            recv_sem=grecv.at[n],
            device_id=(at_offset(dy, dx, dc), part),
            device_id_type=MESH,
        )
        moves[key] = copy
        copy.start()

    first = ((0, 1), (1, 0))
    second = ((1, 0), (0, 1))
    sizes = (count - count // 2, count // 2)
    lows = (0, sizes[0])

    def along(h, i, s=0):
        (py, px), (qy, qx) = first[h], second[h]
        return (i * py + s * qy, i * px + s * qx)

    def send_first(h):
        for s in (1, -1):
            move(("p", h, s), 0, 0, lows[h], sizes[h], *along(h, s))

    def send_second(h, i):
        for s in (1, -1):
            move(("q", h, i, s), *along(h, i), lows[h], sizes[h], *along(h, 0, s))

    def split(h, s):
        near_half = sizes[h] // 2 if h else sizes[h] - sizes[h] // 2
        return (lows[h], near_half) if s > 0 else (lows[h] + near_half, sizes[h] - near_half)

    def forward_first(h, s):
        moves["p", h, s].wait_recv()
        move(("pf", h, s), *along(h, s), *split(h, s), *along(h, s))

    def forward_second(h, i, s):
        moves["q", h, i, s].wait_recv()
        move(("qf", h, i, s), *along(h, i, s), *split(h, s), *along(h, 0, s))

    def to_sibling(oy, ox):
        move(("s", oy % NY, ox % NX), oy, ox, 0, count, 0, 0, 1)

    def add_piece(oy, ox, oc):
        src = at_offset(-oy, -ox, oc)
        buf = piece(oy, ox, oc)
        tiles = []
        for c in range(CAP):
            base = T_IDX + c * TILES
            tiles.append(jnp.concatenate([buf[tab[base + w, src * BLK]] for w in range(TILES)], axis=1))
        out[...] += jnp.dot(lhs_t[src], jnp.concatenate(tiles, axis=0), preferred_element_type=F32)

    def finish(pieces):
        for oy, ox in pieces:
            to_sibling(oy, ox)

    def add(pieces, oc):
        for oy, ox in pieces:
            if oc:
                moves["s", oy % NY, ox % NX].wait_recv()
            add_piece(oy, ox, oc)

    for h in range(2):
        send_first(h)
    for h in range(2):
        send_second(h, 0)
    to_sibling(0, 0)
    for n in range(NG - 1):
        c_copy(n, True).wait_recv()
    z_start(cown, 3)
    for s in (1, -1):
        for h in range(2):
            forward_first(h, s)
            send_second(h, s)
    for s in (1, -1):
        for h in range(2):
            forward_second(h, 0, s)
    near = [(0, 1), (0, -1), (1, 0), (-1, 0)]
    finish(near)
    for h in range(2):
        for s in (1, -1):
            moves["pf", h, s].wait_recv()
        send_second(h, 2)
    diagonal = [(1, 1), (1, -1), (-1, 1), (-1, -1)]
    for i in (1, -1):
        for s in (1, -1):
            for h in range(2):
                forward_second(h, i, s)
    finish(diagonal)
    for h in range(2):
        for s in (1, -1):
            moves["qf", h, 0, s].wait_recv()
    straight = [(0, 2), (2, 0)]
    finish(straight)
    for s in (1, -1):
        for h in range(2):
            forward_second(h, 2, s)
    z_wait_recv(cown, 3)
    lax.fori_loop(0, NG, build, 0)
    for pieces in ([(0, 0)], near, diagonal, straight):
        add(pieces, 0)
        add(pieces, 1)
    for i in (1, -1):
        for h in range(2):
            for s in (1, -1):
                moves["qf", h, i, s].wait_recv()
    knight = [(1, 2), (-1, 2), (2, 1), (2, -1)]
    finish(knight)
    for n in range(NG - 1):
        for h in range(2):
            d_copy(n, h, False).wait_send()
        c_copy(n, False).wait_send()
    z_wait_send(cfull, 0)
    for h in range(2):
        z_wait_send(wz, 6 + 3 * h, (h, 2))
    z_wait_send(cown, 3)
    add(knight, 0)
    add(knight, 1)
    earlier = list(moves.values())
    for h in range(2):
        for s in (1, -1):
            moves["qf", h, 2, s].wait_recv()
        move(("s2", h), 2, 2, lows[h], sizes[h], 0, 0, 1)
    add_piece(2, 2, 0)
    for copy in earlier:
        copy.wait_send()
    for h in range(2):
        moves["s2", h].wait_recv()
    add_piece(2, 2, 1)
    for h in range(2):
        moves["s2", h].wait_send()


def local(colloc, potent, weights, density, list_owner, list_local):
    smem = pl.BlockSpec(memory_space=pltpu.SMEM)
    vmem = pl.BlockSpec(memory_space=pltpu.VMEM)
    tab, keep, few = pl.pallas_call(
        plan_kernel,
        out_shape=(
            jax.ShapeDtypeStruct((T_END, LANES), jnp.int32),
            jax.ShapeDtypeStruct((2 * CAP, LANES), F32),
            jax.ShapeDtypeStruct((1, 1), jnp.int32),
        ),
        in_specs=[vmem, vmem],
        out_specs=(vmem, vmem, smem),
    )(list_owner.T, list_local.T)
    dma = pltpu.SemaphoreType.DMA
    def exchange(count, collective_id):
        return pl.pallas_call(
            functools.partial(kernel, count),
            out_shape=pltpu.VMEM((2 * RBS, TILES * RBS), F32),
            in_specs=[smem, smem, vmem, vmem, vmem, pl.BlockSpec(memory_space=pl.ANY)],
            out_specs=vmem,
            scratch_shapes=[
                pltpu.VMEM((2 * N_COL, RBS, RBS), BF16),
                pltpu.VMEM((NG * CAP, RBS, RBS), BF16),
                pltpu.VMEM((NG * CAP, RBS, RBS), BF16),
                pltpu.VMEM((NG * CAP, RBS, RBS), BF16),
                pltpu.VMEM((NG * CAP, RBS, RBS), BF16),
                pltpu.VMEM((NA * 2 * BLK, RBS, RBS), BF16),
                pltpu.VMEM((NG, CAP, RBS // NA, RBS), BF16),
                pltpu.VMEM((NA * NG, CAP, RBS // NA, RBS), BF16),
                pltpu.VMEM((NA * 2 * BLK, RBS, RBS), BF16),
                pltpu.VMEM((NG, 2 * RBS, CAP * RBS), BF16),
                pltpu.VMEM((RBS, RBS), BF16),
                pltpu.VMEM((2 * BLK, RBS, RBS), F32),
                pltpu.VMEM((2 * RBS, N_COL * RBS), BF16),
            ]
            + [pltpu.VMEM((count + 1, RBS, RBS), BF16)] * NG
            + [
                dma((NG * 2,)),
                dma((NG * 2,)),
                dma((NG,)),
                dma((NG,)),
                dma((6 + 6 * BLK,)),
                dma((6 + 6 * BLK,)),
                dma((80,)),
                dma((80,)),
                dma((2,)),
            ],
            compiler_params=pltpu.CompilerParams(
                collective_id=collective_id, has_side_effects=True, vmem_limit_bytes=56 << 20
            ),
        )

    return lax.cond(
        few[0, 0] > 0,
        exchange(FEW, 0),
        exchange(TILES, 1),
        tab, keep, colloc, potent, weights, density,
    )


def solution(mesh):
    placed = (
        P("grid", None, "ao"),
        P("grid", None, "ao"),
        P("grid", None),
        P("grid", None),
        P(),
        P(),
    )
    return jax.shard_map(
        local, mesh=mesh, in_specs=placed, out_specs=P("grid", "ao"), check_vma=False
    )
```

```python
import functools

import jax
import jax.numpy as jnp
from jax import lax
from jax.experimental import pallas as pl
from jax.experimental.pallas import tpu as pltpu
from jax.sharding import PartitionSpec as P

RBS = 128
SIG = 8
BLK = 4
NG = 32
NA = 4
NY = 4
NX = 4
CAP = 2
TILES = 16
FEW = 13
N_COL = 64
MESH = pl.DeviceIdType.MESH
F32 = jnp.float32
BF16 = jnp.bfloat16

LANES = 128
T_ARR = 0
T_DENS = T_ARR + SIG
T_CB = T_DENS + 2 * CAP
T_SEL = T_CB + 1
T_IDX = 16
T_END = T_IDX + CAP * TILES


def exchange_order():
    far = sorted(
        [(oy, ox, oc) for oy in range(NY) for ox in range(NX) for oc in range(2) if (oy, ox, oc) != (0, 0, 0)],
        key=lambda o: -(min(o[0], NY - o[0]) + min(o[1], NX - o[1])),
    )
    order = []
    for first in far:
        turned = first
        for _ in range(4):
            if turned not in order:
                order.append(turned)
            turned = (turned[1] % NY, -turned[0] % NX, turned[2])
    return order


OFFSETS = exchange_order()


def plan_kernel(own_ref, loc_ref, tab, keep, few):
    me = lax.axis_index("grid")
    part = lax.axis_index("ao")
    i32 = jnp.int32
    own = own_ref[...]
    loc = loc_ref[...]
    shape = (SIG, LANES)
    slot = lax.broadcasted_iota(i32, shape, 0)
    lane = lax.broadcasted_iota(i32, shape, 1)
    block = lane % BLK
    row1 = (1, LANES)
    block1 = lax.broadcasted_iota(i32, row1, 1) % BLK
    row_ids = own * 2 + loc

    def total(v):
        return jnp.sum(v, axis=0, keepdims=True)

    def earlier(v, blk):
        out = jnp.zeros_like(v)
        for s in range(1, BLK):
            out += jnp.where(blk >= s, pltpu.roll(v, s, 1), 0)
        return out

    def over_blocks(v):
        out = v
        for s in range(1, BLK):
            out += pltpu.roll(v, LANES - s, 1)
        return out

    hit = (own == me).astype(i32)
    named = total(hit)
    before = earlier(named, block1)
    row = total(hit * loc)
    cols = [total(jnp.where(slot == part * 2 + h, row_ids, 0)) for h in range(2)]
    chosen = [named * (before == c).astype(i32) for c in range(CAP)]
    for c in range(CAP):
        for h in range(2):
            tab[T_DENS + h * CAP + c, :] = over_blocks(chosen[c] * (row * N_COL + cols[h]))[0]
        for r in range(2):
            keep[c * 2 + r, :] = over_blocks(chosen[c] * (row == r).astype(i32))[0].astype(F32)

    spot = jnp.zeros(shape, i32)
    for s in range(1, BLK):
        prior = pltpu.roll(own, s, 1)
        for j in range(SIG):
            turned = prior if j == 0 else pltpu.roll(prior, j, 0)
            spot += jnp.where((block >= s) & (turned == own), 1, 0)
    arr = own * CAP + spot
    tab[T_ARR : T_ARR + SIG, :] = arr

    group = (own // (NG // NA) == part).astype(i32)
    rank = earlier(total(group), block1) + jnp.zeros(shape, i32)
    for s in range(1, SIG):
        rank += jnp.where(slot >= s, pltpu.roll(group, s, 0), 0)
    to_me = LANES - me * BLK
    my_arr = pltpu.roll(arr, to_me, 1)
    my_rank = pltpu.roll(jnp.where(group > 0, rank, LANES), to_me, 1)
    cb = jnp.zeros(row1, i32)
    sel = jnp.zeros(row1, i32)
    for b in range(BLK):
        at = (slot // 2) * (2 * BLK) + 2 * b + slot % 2
        cb += total(jnp.where(jnp.broadcast_to(my_arr[:, b : b + 1], shape) == lane, at, 0))
        at = (slot // 2) * (2 * BLK) + (slot % 2) * BLK + b
        sel += total(jnp.where(jnp.broadcast_to(my_rank[:, b : b + 1], shape) == lane, at, 0))
    tab[T_CB, :] = cb[0]
    tab[T_SEL, :] = sel[0]
    for n in range(TILES):
        at = total(jnp.where(row_ids == part * TILES + n, rank + 1, 0))
        for c in range(CAP):
            tab[T_IDX + c * TILES + n, :] = over_blocks(chosen[c] * at)[0]

    most = jnp.zeros(row1, i32)
    for z in range(NA):
        most = jnp.maximum(most, over_blocks(total((own // (NG // NA) == z).astype(i32))))
    most = jnp.where(block1 == 0, most, 0)
    few[0, 0] = (jnp.max(most) <= FEW).astype(i32)


def kernel(count, tab, keep, colloc, potent, weights, dens, out, dtiles, send0, send1, arrived0, arrived1, cfull, cqs, cown, wz, lhs_t, picked, scaled, dloc, *rest):
    held = rest[: NG]
    dsend, drecv, csend, crecv, zsend, zrecv, gsend, grecv, lsem = rest[NG:]
    me = lax.axis_index("grid")
    part = lax.axis_index("ao")
    y = me // (2 * NX)
    x = (me // 2) % NX
    core = me % 2

    def at_offset(oy, ox, oc):
        return ((y + oy + NY) % NY) * (2 * NX) + ((x + ox + NX) % NX) * 2 + (core + oc) % 2

    rows_in = [
        pltpu.make_async_copy(dens.at[pl.ds(r * RBS, RBS)], dloc.at[pl.ds(r * RBS, RBS)], lsem.at[r]) for r in range(2)
    ]
    for copy in rows_in:
        copy.start()
    barrier = pltpu.get_barrier_semaphore()
    for o in OFFSETS:
        pl.semaphore_signal(barrier, inc=1, device_id=(at_offset(*o), part), device_id_type=MESH)
    for o in range(1, NA):
        pl.semaphore_signal(barrier, inc=1, device_id=(me, (part + o) % NA), device_id_type=MESH)

    send = (send0, send1)
    arrived = (arrived0, arrived1)

    def pack(h):
        def step(d, carry):
            for c in range(CAP):
                send[h][d * CAP + c] = dtiles[tab[T_DENS + h * CAP + c, d * BLK]]
            return carry

        lax.fori_loop(0, NG, step, 0)

    for r in range(2):
        rows_in[r].wait()
        for k in range(N_COL):
            dtiles[r * N_COL + k] = dloc[r * RBS : (r + 1) * RBS, k * RBS : (k + 1) * RBS]
    pack(0)
    for b in range(BLK):
        for h in range(2):
            cfull[part * 2 * BLK + 2 * b + h] = colloc[b, :, h * RBS : (h + 1) * RBS]
    pl.semaphore_wait(barrier, len(OFFSETS) + NA - 1)

    def z_copy(buf, base, o, there, cut=(0, 1)):
        whole = buf.shape[0] // NA
        count = whole // cut[1]
        low = cut[0] * count
        return pltpu.make_async_remote_copy(
            src_ref=buf.at[pl.ds(part * whole + low, count)],
            dst_ref=buf.at[pl.ds(there * whole + low, count)],
            send_sem=zsend.at[base + o - 1],
            recv_sem=zrecv.at[base + o - 1],
            device_id=(me, (part + o) % NA),
            device_id_type=MESH,
        )

    def z_start(buf, base, cut=(0, 1)):
        for o in (2, 1, 3):
            z_copy(buf, base, o, part, cut).start()

    def z_wait_recv(buf, base, cut=(0, 1)):
        for o in (1, 3, 2):
            z_copy(buf, base, o, (part + NA - o) % NA, cut).wait_recv()

    def z_wait_send(buf, base, cut=(0, 1)):
        for o in (1, 2, 3):
            z_copy(buf, base, o, part, cut).wait_send()

    def d_copy(n, h, recv):
        oy, ox, oc = OFFSETS[n]
        to = at_offset(oy, ox, oc)
        frm = at_offset(-oy, -ox, oc) if recv else me
        return pltpu.make_async_remote_copy(
            src_ref=send[h].at[pl.ds(to * CAP, CAP)],
            dst_ref=arrived[h].at[pl.ds(frm * CAP, CAP)],
            send_sem=dsend.at[n * 2 + h],
            recv_sem=drecv.at[n * 2 + h],
            device_id=(to, part),
            device_id_type=MESH,
        )

    def c_copy(n, recv):
        oy, ox, oc = OFFSETS[n]
        to = at_offset(oy, ox, oc)
        frm = at_offset(-oy, -ox, oc) if recv else me
        return pltpu.make_async_remote_copy(
            src_ref=cqs.at[to],
            dst_ref=cown.at[part * NG + frm],
            send_sem=csend.at[n],
            recv_sem=crecv.at[n],
            device_id=(to, part),
            device_id_type=MESH,
        )

    z_start(cfull, 0)
    for n in range(NG - 1):
        d_copy(n, 0, False).start()
    pack(1)
    for n in range(NG - 1):
        d_copy(n, 1, False).start()
    for h in range(2):
        for c in range(CAP):
            arrived[h][me * CAP + c] = send[h][me * CAP + c]
    for b in range(BLK):
        w = jnp.transpose(jnp.broadcast_to(weights[b : b + 1, :], (RBS, RBS)))
        for h in range(2):
            scaled[h * BLK + b] = w * potent[b, :, h * RBS : (h + 1) * RBS].astype(F32)
    for s in range(NG):
        held[s][0] = jnp.zeros((RBS, RBS), BF16)
    out[...] = jnp.zeros_like(out)

    z_wait_recv(cfull, 0)
    quarter = RBS // NA

    def pack_c(o, carry):
        for c in range(CAP):
            picked[...] = cfull[tab[T_CB, o * CAP + c]]
            rows = pl.multiple_of(part * quarter, quarter)
            cqs[o, c] = picked[pl.ds(rows, quarter), :]
        return carry

    lax.fori_loop(0, NG, pack_c, 0)
    cown[part * NG + me] = cqs[me]

    for h in range(2):
        for n in range(NG - 1):
            d_copy(n, h, True).wait_recv()
        for b in range(BLK):
            left = jnp.concatenate([cfull[q * 2 * BLK + 2 * b + g] for q in range(NA) for g in range(2)], axis=1)
            right = jnp.concatenate([arrived[h][tab[T_ARR + j, me * BLK + b]] for j in range(SIG)], axis=0)
            f_vals = jnp.dot(left, right, preferred_element_type=F32)
            wz[part * 2 * BLK + h * BLK + b] = (scaled[h * BLK + b] * f_vals).astype(BF16)
        z_start(wz, 6 + 3 * h, (h, 2))
    for n in range(NG - 1):
        c_copy(n, False).start()
    for h in range(2):
        z_wait_recv(wz, 6 + 3 * h, (h, 2))

    def build(d, carry):
        for c in range(CAP):
            tile = jnp.concatenate([cown[q * NG + d, c].astype(F32) for q in range(NA)], axis=0)
            tile = jnp.transpose(tile)
            for r in range(2):
                lhs_t[d, r * RBS : (r + 1) * RBS, c * RBS : (c + 1) * RBS] = (
                    tile * keep[c * 2 + r, d * BLK]
                ).astype(BF16)
        return carry

    def piece(oy, ox, oc=0):
        return held[((oy % NY) * NX + ox % NX) * 2 + oc]

    own = piece(0, 0)
    for t in range(count):
        own[1 + t] = wz[tab[T_SEL, t]]

    moves = {}

    def move(key, oy, ox, low, size, dy, dx, dc=0):
        n = len(moves)
        rows = pl.ds(1 + low, size)
        copy = pltpu.make_async_remote_copy(
            src_ref=piece(oy, ox).at[rows],
            dst_ref=piece(oy + dy, ox + dx, dc).at[rows],
            send_sem=gsend.at[n],
            recv_sem=grecv.at[n],
            device_id=(at_offset(dy, dx, dc), part),
            device_id_type=MESH,
        )
        moves[key] = copy
        copy.start()

    first = ((0, 1), (1, 0))
    second = ((1, 0), (0, 1))
    sizes = (count - count // 2, count // 2)
    lows = (0, sizes[0])

    def along(h, i, s=0):
        (py, px), (qy, qx) = first[h], second[h]
        return (i * py + s * qy, i * px + s * qx)

    def send_first(h):
        for s in (1, -1):
            move(("p", h, s), 0, 0, lows[h], sizes[h], *along(h, s))

    def send_second(h, i):
        for s in (1, -1):
            move(("q", h, i, s), *along(h, i), lows[h], sizes[h], *along(h, 0, s))

    def split(h, s):
        near_half = sizes[h] // 2 if h else sizes[h] - sizes[h] // 2
        return (lows[h], near_half) if s > 0 else (lows[h] + near_half, sizes[h] - near_half)

    def forward_first(h, s):
        moves["p", h, s].wait_recv()
        move(("pf", h, s), *along(h, s), *split(h, s), *along(h, s))

    def forward_second(h, i, s):
        moves["q", h, i, s].wait_recv()
        move(("qf", h, i, s), *along(h, i, s), *split(h, s), *along(h, 0, s))

    def to_sibling(oy, ox):
        move(("s", oy % NY, ox % NX), oy, ox, 0, count, 0, 0, 1)

    def half_to_sibling(h, oy, ox):
        move(("s", h, oy % NY, ox % NX), oy, ox, lows[h], sizes[h], 0, 0, 1)

    def add_piece(oy, ox, oc):
        src = at_offset(-oy, -ox, oc)
        buf = piece(oy, ox, oc)
        tiles = []
        for c in range(CAP):
            base = T_IDX + c * TILES
            tiles.append(jnp.concatenate([buf[tab[base + w, src * BLK]] for w in range(TILES)], axis=1))
        out[...] += jnp.dot(lhs_t[src], jnp.concatenate(tiles, axis=0), preferred_element_type=F32)

    def finish(pieces):
        for oy, ox in pieces:
            to_sibling(oy, ox)

    def add(pieces, oc):
        for oy, ox in pieces:
            if oc:
                if (oy, ox) in knight:
                    for h in range(2):
                        moves["s", h, oy % NY, ox % NX].wait_recv()
                else:
                    moves["s", oy % NY, ox % NX].wait_recv()
            add_piece(oy, ox, oc)

    for h in range(2):
        send_first(h)
    for h in range(2):
        send_second(h, 0)
    to_sibling(0, 0)
    for n in range(NG - 1):
        c_copy(n, True).wait_recv()
    z_start(cown, 3)
    for s in (1, -1):
        for h in range(2):
            forward_first(h, s)
            send_second(h, s)
    for s in (1, -1):
        for h in range(2):
            forward_second(h, 0, s)
    near = [(0, 1), (0, -1), (1, 0), (-1, 0)]
    finish(near)
    for h in range(2):
        for s in (1, -1):
            moves["pf", h, s].wait_recv()
        send_second(h, 2)
    diagonal = [(1, 1), (1, -1), (-1, 1), (-1, -1)]
    for i in (1, -1):
        for s in (1, -1):
            for h in range(2):
                forward_second(h, i, s)
    finish(diagonal)
    for h in range(2):
        for s in (1, -1):
            moves["qf", h, 0, s].wait_recv()
    straight = [(0, 2), (2, 0)]
    knight = [(1, 2), (-1, 2), (2, 1), (2, -1)]
    finish(straight)
    for s in (1, -1):
        for h in range(2):
            forward_second(h, 2, s)
            half_to_sibling(h, *along(h, 2, s))
    z_wait_recv(cown, 3)
    lax.fori_loop(0, NG, build, 0)
    for pieces in ([(0, 0)], near, diagonal, straight):
        add(pieces, 0)
        add(pieces, 1)
    for i in (1, -1):
        for h in range(2):
            for s in (1, -1):
                moves["qf", h, i, s].wait_recv()
            half_to_sibling(h, *along(h, i, 2))
    for n in range(NG - 1):
        for h in range(2):
            d_copy(n, h, False).wait_send()
        c_copy(n, False).wait_send()
    z_wait_send(cfull, 0)
    for h in range(2):
        z_wait_send(wz, 6 + 3 * h, (h, 2))
    z_wait_send(cown, 3)
    earlier = list(moves.values())
    for h in range(2):
        for s in (1, -1):
            moves["qf", h, 2, s].wait_recv()
        move(("s2", h), 2, 2, lows[h], sizes[h], 0, 0, 1)
    add(knight, 0)
    add_piece(2, 2, 0)
    add(knight, 1)
    for copy in earlier:
        copy.wait_send()
    for h in range(2):
        moves["s2", h].wait_recv()
    add_piece(2, 2, 1)
    for h in range(2):
        moves["s2", h].wait_send()


def local(colloc, potent, weights, density, list_owner, list_local):
    smem = pl.BlockSpec(memory_space=pltpu.SMEM)
    vmem = pl.BlockSpec(memory_space=pltpu.VMEM)
    tab, keep, few = pl.pallas_call(
        plan_kernel,
        out_shape=(
            jax.ShapeDtypeStruct((T_END, LANES), jnp.int32),
            jax.ShapeDtypeStruct((2 * CAP, LANES), F32),
            jax.ShapeDtypeStruct((1, 1), jnp.int32),
        ),
        in_specs=[vmem, vmem],
        out_specs=(vmem, vmem, smem),
    )(list_owner.T, list_local.T)
    dma = pltpu.SemaphoreType.DMA
    def exchange(count, collective_id):
        return pl.pallas_call(
            functools.partial(kernel, count),
            out_shape=pltpu.VMEM((2 * RBS, TILES * RBS), F32),
            in_specs=[smem, smem, vmem, vmem, vmem, pl.BlockSpec(memory_space=pl.ANY)],
            out_specs=vmem,
            scratch_shapes=[
                pltpu.VMEM((2 * N_COL, RBS, RBS), BF16),
                pltpu.VMEM((NG * CAP, RBS, RBS), BF16),
                pltpu.VMEM((NG * CAP, RBS, RBS), BF16),
                pltpu.VMEM((NG * CAP, RBS, RBS), BF16),
                pltpu.VMEM((NG * CAP, RBS, RBS), BF16),
                pltpu.VMEM((NA * 2 * BLK, RBS, RBS), BF16),
                pltpu.VMEM((NG, CAP, RBS // NA, RBS), BF16),
                pltpu.VMEM((NA * NG, CAP, RBS // NA, RBS), BF16),
                pltpu.VMEM((NA * 2 * BLK, RBS, RBS), BF16),
                pltpu.VMEM((NG, 2 * RBS, CAP * RBS), BF16),
                pltpu.VMEM((RBS, RBS), BF16),
                pltpu.VMEM((2 * BLK, RBS, RBS), F32),
                pltpu.VMEM((2 * RBS, N_COL * RBS), BF16),
            ]
            + [pltpu.VMEM((count + 1, RBS, RBS), BF16)] * NG
            + [
                dma((NG * 2,)),
                dma((NG * 2,)),
                dma((NG,)),
                dma((NG,)),
                dma((6 + 6 * BLK,)),
                dma((6 + 6 * BLK,)),
                dma((80,)),
                dma((80,)),
                dma((2,)),
            ],
            compiler_params=pltpu.CompilerParams(
                collective_id=collective_id, has_side_effects=True, vmem_limit_bytes=56 << 20
            ),
        )

    return lax.cond(
        few[0, 0] > 0,
        exchange(FEW, 0),
        exchange(TILES, 1),
        tab, keep, colloc, potent, weights, density,
    )


def solution(mesh):
    placed = (
        P("grid", None, "ao"),
        P("grid", None, "ao"),
        P("grid", None),
        P("grid", None),
        P(),
        P(),
    )
    return jax.shard_map(
        local, mesh=mesh, in_specs=placed, out_specs=P("grid", "ao"), check_vma=False
    )
```

```python
import functools

import jax
import jax.numpy as jnp
from jax import lax
from jax.experimental import pallas as pl
from jax.experimental.pallas import tpu as pltpu
from jax.sharding import PartitionSpec as P

RBS = 128
SIG = 8
BLK = 4
NG = 32
NA = 4
NY = 4
NX = 4
CAP = 2
TILES = 16
FEW = 13
FEWER = 12
N_COL = 64
MESH = pl.DeviceIdType.MESH
F32 = jnp.float32
BF16 = jnp.bfloat16

LANES = 128
T_ARR = 0
T_DENS = T_ARR + SIG
T_CB = T_DENS + 2 * CAP
T_SEL = T_CB + 1
T_IDX = 16
T_END = T_IDX + CAP * TILES


def exchange_order():
    far = sorted(
        [(oy, ox, oc) for oy in range(NY) for ox in range(NX) for oc in range(2) if (oy, ox, oc) != (0, 0, 0)],
        key=lambda o: -(min(o[0], NY - o[0]) + min(o[1], NX - o[1])),
    )
    order = []
    for first in far:
        turned = first
        for _ in range(4):
            if turned not in order:
                order.append(turned)
            turned = (turned[1] % NY, -turned[0] % NX, turned[2])
    return order


OFFSETS = exchange_order()


def plan_kernel(own_ref, loc_ref, tab, keep, few):
    me = lax.axis_index("grid")
    part = lax.axis_index("ao")
    i32 = jnp.int32
    own = own_ref[...]
    loc = loc_ref[...]
    shape = (SIG, LANES)
    slot = lax.broadcasted_iota(i32, shape, 0)
    lane = lax.broadcasted_iota(i32, shape, 1)
    block = lane % BLK
    row1 = (1, LANES)
    block1 = lax.broadcasted_iota(i32, row1, 1) % BLK
    row_ids = own * 2 + loc

    def total(v):
        return jnp.sum(v, axis=0, keepdims=True)

    def earlier(v, blk):
        out = jnp.zeros_like(v)
        for s in range(1, BLK):
            out += jnp.where(blk >= s, pltpu.roll(v, s, 1), 0)
        return out

    def over_blocks(v):
        out = v
        for s in range(1, BLK):
            out += pltpu.roll(v, LANES - s, 1)
        return out

    hit = (own == me).astype(i32)
    named = total(hit)
    before = earlier(named, block1)
    row = total(hit * loc)
    cols = [total(jnp.where(slot == part * 2 + h, row_ids, 0)) for h in range(2)]
    chosen = [named * (before == c).astype(i32) for c in range(CAP)]
    for c in range(CAP):
        for h in range(2):
            tab[T_DENS + h * CAP + c, :] = over_blocks(chosen[c] * (row * N_COL + cols[h]))[0]
        for r in range(2):
            keep[c * 2 + r, :] = over_blocks(chosen[c] * (row == r).astype(i32))[0].astype(F32)

    spot = jnp.zeros(shape, i32)
    for s in range(1, BLK):
        prior = pltpu.roll(own, s, 1)
        for j in range(SIG):
            turned = prior if j == 0 else pltpu.roll(prior, j, 0)
            spot += jnp.where((block >= s) & (turned == own), 1, 0)
    arr = own * CAP + spot
    tab[T_ARR : T_ARR + SIG, :] = arr

    group = (own // (NG // NA) == part).astype(i32)
    rank = earlier(total(group), block1) + jnp.zeros(shape, i32)
    for s in range(1, SIG):
        rank += jnp.where(slot >= s, pltpu.roll(group, s, 0), 0)
    to_me = LANES - me * BLK
    my_arr = pltpu.roll(arr, to_me, 1)
    my_rank = pltpu.roll(jnp.where(group > 0, rank, LANES), to_me, 1)
    cb = jnp.zeros(row1, i32)
    sel = jnp.zeros(row1, i32)
    for b in range(BLK):
        at = (slot // 2) * (2 * BLK) + 2 * b + slot % 2
        cb += total(jnp.where(jnp.broadcast_to(my_arr[:, b : b + 1], shape) == lane, at, 0))
        at = (slot // 2) * (2 * BLK) + (slot % 2) * BLK + b
        sel += total(jnp.where(jnp.broadcast_to(my_rank[:, b : b + 1], shape) == lane, at, 0))
    tab[T_CB, :] = cb[0]
    tab[T_SEL, :] = sel[0]
    for n in range(TILES):
        at = total(jnp.where(row_ids == part * TILES + n, rank + 1, 0))
        for c in range(CAP):
            tab[T_IDX + c * TILES + n, :] = over_blocks(chosen[c] * at)[0]

    most = jnp.zeros(row1, i32)
    for z in range(NA):
        most = jnp.maximum(most, over_blocks(total((own // (NG // NA) == z).astype(i32))))
    most = jnp.where(block1 == 0, most, 0)
    highest = jnp.max(most)
    few[0, 0] = (highest <= FEW).astype(i32) + (highest <= FEWER).astype(i32)


def kernel(count, tab, keep, colloc, potent, weights, dens, out, dtiles, send0, send1, arrived0, arrived1, cfull, cqs, cown, wz, lhs_t, picked, scaled, dloc, *rest):
    held = rest[: NG]
    dsend, drecv, csend, crecv, zsend, zrecv, gsend, grecv, lsem = rest[NG:]
    me = lax.axis_index("grid")
    part = lax.axis_index("ao")
    y = me // (2 * NX)
    x = (me // 2) % NX
    core = me % 2

    def at_offset(oy, ox, oc):
        return ((y + oy + NY) % NY) * (2 * NX) + ((x + ox + NX) % NX) * 2 + (core + oc) % 2

    rows_in = [
        pltpu.make_async_copy(dens.at[pl.ds(r * RBS, RBS)], dloc.at[pl.ds(r * RBS, RBS)], lsem.at[r]) for r in range(2)
    ]
    for copy in rows_in:
        copy.start()
    barrier = pltpu.get_barrier_semaphore()
    for o in OFFSETS:
        pl.semaphore_signal(barrier, inc=1, device_id=(at_offset(*o), part), device_id_type=MESH)
    for o in range(1, NA):
        pl.semaphore_signal(barrier, inc=1, device_id=(me, (part + o) % NA), device_id_type=MESH)

    send = (send0, send1)
    arrived = (arrived0, arrived1)

    def pack(h):
        def step(d, carry):
            for c in range(CAP):
                send[h][d * CAP + c] = dtiles[tab[T_DENS + h * CAP + c, d * BLK]]
            return carry

        lax.fori_loop(0, NG, step, 0)

    for r in range(2):
        rows_in[r].wait()
        for k in range(N_COL):
            dtiles[r * N_COL + k] = dloc[r * RBS : (r + 1) * RBS, k * RBS : (k + 1) * RBS]
    pack(0)
    for b in range(BLK):
        for h in range(2):
            cfull[part * 2 * BLK + 2 * b + h] = colloc[b, :, h * RBS : (h + 1) * RBS]
    pl.semaphore_wait(barrier, len(OFFSETS) + NA - 1)

    def z_copy(buf, base, o, there, cut=(0, 1)):
        whole = buf.shape[0] // NA
        count = whole // cut[1]
        low = cut[0] * count
        return pltpu.make_async_remote_copy(
            src_ref=buf.at[pl.ds(part * whole + low, count)],
            dst_ref=buf.at[pl.ds(there * whole + low, count)],
            send_sem=zsend.at[base + o - 1],
            recv_sem=zrecv.at[base + o - 1],
            device_id=(me, (part + o) % NA),
            device_id_type=MESH,
        )

    def z_start(buf, base, cut=(0, 1)):
        for o in (2, 1, 3):
            z_copy(buf, base, o, part, cut).start()

    def z_wait_recv(buf, base, cut=(0, 1)):
        for o in (1, 3, 2):
            z_copy(buf, base, o, (part + NA - o) % NA, cut).wait_recv()

    def z_wait_send(buf, base, cut=(0, 1)):
        for o in (1, 2, 3):
            z_copy(buf, base, o, part, cut).wait_send()

    def d_copy(n, h, recv):
        oy, ox, oc = OFFSETS[n]
        to = at_offset(oy, ox, oc)
        frm = at_offset(-oy, -ox, oc) if recv else me
        return pltpu.make_async_remote_copy(
            src_ref=send[h].at[pl.ds(to * CAP, CAP)],
            dst_ref=arrived[h].at[pl.ds(frm * CAP, CAP)],
            send_sem=dsend.at[n * 2 + h],
            recv_sem=drecv.at[n * 2 + h],
            device_id=(to, part),
            device_id_type=MESH,
        )

    def c_copy(n, recv):
        oy, ox, oc = OFFSETS[n]
        to = at_offset(oy, ox, oc)
        frm = at_offset(-oy, -ox, oc) if recv else me
        return pltpu.make_async_remote_copy(
            src_ref=cqs.at[to],
            dst_ref=cown.at[part * NG + frm],
            send_sem=csend.at[n],
            recv_sem=crecv.at[n],
            device_id=(to, part),
            device_id_type=MESH,
        )

    z_start(cfull, 0)
    for n in range(NG - 1):
        d_copy(n, 0, False).start()
    pack(1)
    for n in range(NG - 1):
        d_copy(n, 1, False).start()
    for h in range(2):
        for c in range(CAP):
            arrived[h][me * CAP + c] = send[h][me * CAP + c]
    for b in range(BLK):
        w = jnp.transpose(jnp.broadcast_to(weights[b : b + 1, :], (RBS, RBS)))
        for h in range(2):
            scaled[h * BLK + b] = w * potent[b, :, h * RBS : (h + 1) * RBS].astype(F32)
    for s in range(NG):
        held[s][0] = jnp.zeros((RBS, RBS), BF16)
    out[...] = jnp.zeros_like(out)

    z_wait_recv(cfull, 0)
    quarter = RBS // NA

    def pack_c(o, carry):
        for c in range(CAP):
            picked[...] = cfull[tab[T_CB, o * CAP + c]]
            rows = pl.multiple_of(part * quarter, quarter)
            cqs[o, c] = picked[pl.ds(rows, quarter), :]
        return carry

    lax.fori_loop(0, NG, pack_c, 0)
    cown[part * NG + me] = cqs[me]

    for h in range(2):
        for n in range(NG - 1):
            d_copy(n, h, True).wait_recv()
        for b in range(BLK):
            left = jnp.concatenate([cfull[q * 2 * BLK + 2 * b + g] for q in range(NA) for g in range(2)], axis=1)
            right = jnp.concatenate([arrived[h][tab[T_ARR + j, me * BLK + b]] for j in range(SIG)], axis=0)
            f_vals = jnp.dot(left, right, preferred_element_type=F32)
            wz[part * 2 * BLK + h * BLK + b] = (scaled[h * BLK + b] * f_vals).astype(BF16)
        z_start(wz, 6 + 3 * h, (h, 2))
    for n in range(NG - 1):
        c_copy(n, False).start()
    for h in range(2):
        z_wait_recv(wz, 6 + 3 * h, (h, 2))

    def build(d, carry):
        for c in range(CAP):
            tile = jnp.concatenate([cown[q * NG + d, c].astype(F32) for q in range(NA)], axis=0)
            tile = jnp.transpose(tile)
            for r in range(2):
                lhs_t[d, r * RBS : (r + 1) * RBS, c * RBS : (c + 1) * RBS] = (
                    tile * keep[c * 2 + r, d * BLK]
                ).astype(BF16)
        return carry

    def piece(oy, ox, oc=0):
        return held[((oy % NY) * NX + ox % NX) * 2 + oc]

    own = piece(0, 0)
    for t in range(count):
        own[1 + t] = wz[tab[T_SEL, t]]

    moves = {}

    def move(key, oy, ox, low, size, dy, dx, dc=0):
        n = len(moves)
        rows = pl.ds(1 + low, size)
        copy = pltpu.make_async_remote_copy(
            src_ref=piece(oy, ox).at[rows],
            dst_ref=piece(oy + dy, ox + dx, dc).at[rows],
            send_sem=gsend.at[n],
            recv_sem=grecv.at[n],
            device_id=(at_offset(dy, dx, dc), part),
            device_id_type=MESH,
        )
        moves[key] = copy
        copy.start()

    first = ((0, 1), (1, 0))
    second = ((1, 0), (0, 1))
    sizes = (count - count // 2, count // 2)
    lows = (0, sizes[0])

    def along(h, i, s=0):
        (py, px), (qy, qx) = first[h], second[h]
        return (i * py + s * qy, i * px + s * qx)

    def send_first(h):
        for s in (1, -1):
            move(("p", h, s), 0, 0, lows[h], sizes[h], *along(h, s))

    def send_second(h, i):
        for s in (1, -1):
            move(("q", h, i, s), *along(h, i), lows[h], sizes[h], *along(h, 0, s))

    def split(h, s):
        near_half = sizes[h] // 2 if h else sizes[h] - sizes[h] // 2
        return (lows[h], near_half) if s > 0 else (lows[h] + near_half, sizes[h] - near_half)

    def forward_first(h, s):
        moves["p", h, s].wait_recv()
        move(("pf", h, s), *along(h, s), *split(h, s), *along(h, s))

    def forward_second(h, i, s):
        moves["q", h, i, s].wait_recv()
        move(("qf", h, i, s), *along(h, i, s), *split(h, s), *along(h, 0, s))

    def to_sibling(oy, ox):
        move(("s", oy % NY, ox % NX), oy, ox, 0, count, 0, 0, 1)

    def half_to_sibling(h, oy, ox):
        move(("s", h, oy % NY, ox % NX), oy, ox, lows[h], sizes[h], 0, 0, 1)

    def add_piece(oy, ox, oc):
        src = at_offset(-oy, -ox, oc)
        buf = piece(oy, ox, oc)
        tiles = []
        for c in range(CAP):
            base = T_IDX + c * TILES
            tiles.append(jnp.concatenate([buf[tab[base + w, src * BLK]] for w in range(TILES)], axis=1))
        out[...] += jnp.dot(lhs_t[src], jnp.concatenate(tiles, axis=0), preferred_element_type=F32)

    def finish(pieces):
        for oy, ox in pieces:
            to_sibling(oy, ox)

    def add(pieces, oc):
        for oy, ox in pieces:
            if oc:
                if (oy, ox) in knight:
                    for h in range(2):
                        moves["s", h, oy % NY, ox % NX].wait_recv()
                else:
                    moves["s", oy % NY, ox % NX].wait_recv()
            add_piece(oy, ox, oc)

    for h in range(2):
        send_first(h)
    for h in range(2):
        send_second(h, 0)
    to_sibling(0, 0)
    for n in range(NG - 1):
        c_copy(n, True).wait_recv()
    z_start(cown, 3)
    for s in (1, -1):
        for h in range(2):
            forward_first(h, s)
            send_second(h, s)
    for s in (1, -1):
        for h in range(2):
            forward_second(h, 0, s)
    near = [(0, 1), (0, -1), (1, 0), (-1, 0)]
    finish(near)
    for h in range(2):
        for s in (1, -1):
            moves["pf", h, s].wait_recv()
        send_second(h, 2)
    diagonal = [(1, 1), (1, -1), (-1, 1), (-1, -1)]
    for i in (1, -1):
        for s in (1, -1):
            for h in range(2):
                forward_second(h, i, s)
    finish(diagonal)
    for h in range(2):
        for s in (1, -1):
            moves["qf", h, 0, s].wait_recv()
    straight = [(0, 2), (2, 0)]
    knight = [(1, 2), (-1, 2), (2, 1), (2, -1)]
    finish(straight)
    for s in (1, -1):
        for h in range(2):
            forward_second(h, 2, s)
            half_to_sibling(h, *along(h, 2, s))
    z_wait_recv(cown, 3)
    lax.fori_loop(0, NG, build, 0)
    for pieces in ([(0, 0)], near, diagonal, straight):
        add(pieces, 0)
        add(pieces, 1)
    for i in (1, -1):
        for h in range(2):
            for s in (1, -1):
                moves["qf", h, i, s].wait_recv()
            half_to_sibling(h, *along(h, i, 2))
    for n in range(NG - 1):
        for h in range(2):
            d_copy(n, h, False).wait_send()
        c_copy(n, False).wait_send()
    z_wait_send(cfull, 0)
    for h in range(2):
        z_wait_send(wz, 6 + 3 * h, (h, 2))
    z_wait_send(cown, 3)
    earlier = list(moves.values())
    for h in range(2):
        for s in (1, -1):
            moves["qf", h, 2, s].wait_recv()
        move(("s2", h), 2, 2, lows[h], sizes[h], 0, 0, 1)
    add(knight, 0)
    add_piece(2, 2, 0)
    add(knight, 1)
    for copy in earlier:
        copy.wait_send()
    for h in range(2):
        moves["s2", h].wait_recv()
    add_piece(2, 2, 1)
    for h in range(2):
        moves["s2", h].wait_send()


def local(colloc, potent, weights, density, list_owner, list_local):
    smem = pl.BlockSpec(memory_space=pltpu.SMEM)
    vmem = pl.BlockSpec(memory_space=pltpu.VMEM)
    tab, keep, few = pl.pallas_call(
        plan_kernel,
        out_shape=(
            jax.ShapeDtypeStruct((T_END, LANES), jnp.int32),
            jax.ShapeDtypeStruct((2 * CAP, LANES), F32),
            jax.ShapeDtypeStruct((1, 1), jnp.int32),
        ),
        in_specs=[vmem, vmem],
        out_specs=(vmem, vmem, smem),
    )(list_owner.T, list_local.T)
    dma = pltpu.SemaphoreType.DMA
    def exchange(count, collective_id):
        return pl.pallas_call(
            functools.partial(kernel, count),
            out_shape=pltpu.VMEM((2 * RBS, TILES * RBS), F32),
            in_specs=[smem, smem, vmem, vmem, vmem, pl.BlockSpec(memory_space=pl.ANY)],
            out_specs=vmem,
            scratch_shapes=[
                pltpu.VMEM((2 * N_COL, RBS, RBS), BF16),
                pltpu.VMEM((NG * CAP, RBS, RBS), BF16),
                pltpu.VMEM((NG * CAP, RBS, RBS), BF16),
                pltpu.VMEM((NG * CAP, RBS, RBS), BF16),
                pltpu.VMEM((NG * CAP, RBS, RBS), BF16),
                pltpu.VMEM((NA * 2 * BLK, RBS, RBS), BF16),
                pltpu.VMEM((NG, CAP, RBS // NA, RBS), BF16),
                pltpu.VMEM((NA * NG, CAP, RBS // NA, RBS), BF16),
                pltpu.VMEM((NA * 2 * BLK, RBS, RBS), BF16),
                pltpu.VMEM((NG, 2 * RBS, CAP * RBS), BF16),
                pltpu.VMEM((RBS, RBS), BF16),
                pltpu.VMEM((2 * BLK, RBS, RBS), F32),
                pltpu.VMEM((2 * RBS, N_COL * RBS), BF16),
            ]
            + [pltpu.VMEM((count + 1, RBS, RBS), BF16)] * NG
            + [
                dma((NG * 2,)),
                dma((NG * 2,)),
                dma((NG,)),
                dma((NG,)),
                dma((6 + 6 * BLK,)),
                dma((6 + 6 * BLK,)),
                dma((80,)),
                dma((80,)),
                dma((2,)),
            ],
            compiler_params=pltpu.CompilerParams(
                collective_id=collective_id, has_side_effects=True, vmem_limit_bytes=56 << 20
            ),
        )

    return lax.switch(
        few[0, 0],
        [exchange(TILES, 1), exchange(FEW, 0), exchange(FEWER, 2)],
        tab, keep, colloc, potent, weights, density,
    )


def solution(mesh):
    placed = (
        P("grid", None, "ao"),
        P("grid", None, "ao"),
        P("grid", None),
        P("grid", None),
        P(),
        P(),
    )
    return jax.shard_map(
        local, mesh=mesh, in_specs=placed, out_specs=P("grid", "ao"), check_vma=False
    )
```
